256 devices in a mesh: lon: 32 (over z, x_hi, core), lat: 8 (over y, x_lo).
Axes of the slice: x: 4 (x_hi: 2, x_lo: 2; x = x_hi * 2 + x_lo), y: 4, z: 8, core: 2. Of those that a mesh axis runs over, the one named last changes fastest.
Arguments:
- increment: float32 [512, 512, 256], P('lat', 'lon'), may hold values from -8 to 8
- error_std: float32 [512, 512, 256], P('lat', 'lon'), may hold values from 0.3 to 3
- vertical: float32 [4, 64, 64], replicated, may hold values from -0.75 to 0.75
- lon_decay: float32 [512, 256], P('lon'), may hold values from 0 to 1, as said below
- lat_decay: float32 [512, 256], P('lat'), may hold values from 0 to 1, as said below
Outputs:
- result_field: float32 [512, 512, 256], P('lat', 'lon')
The draws below stay inside these ranges and needn't reach their ends.
Inputs may be any that keep to these rules, and one draw needn't show every extreme that they name: `lon_decay`: every entry is positive and below 1 - 0.07 / 512. `lat_decay`: every entry is positive and below 1.
All inputs are finite; a program needn't handle non-finite values.
Results may differ from the reference program's by a relative error of at most 0.0003.
Values sent between devices are 32-bit elements; how exact they have to be, the bound alone decides.
A program may use at most 128 MiB of HBM per device.

```python
import math
import jax
import jax.numpy as jnp
from jax import lax

NVAR = 4
NLEV = 64
KV = 256
NLAT = 512
NLON = 512


def decay_table(key, gridcell_count, channels, rate_top):
    child_keys = jax.random.split(key, 4)
    baseline_rate = jnp.exp(jax.random.uniform(child_keys[0], (1, channels), jnp.float32, math.log(0.15 / gridcell_count), math.log(rate_top)))
    noisy_component = jnp.exp(jax.random.uniform(child_keys[1], (gridcell_count, channels), jnp.float32, math.log(0.5), math.log(2.0)))
    spike_events = jax.random.randint(child_keys[2], (gridcell_count, 1), 0, gridcell_count) < 4
    spike_penalty = jax.random.uniform(child_keys[3], (gridcell_count, 1), jnp.float32, 0.5, 0.8)
    return jnp.exp(-baseline_rate * noisy_component) * jnp.where(spike_events, spike_penalty, 1.0)


def draw_lon_decay(key, part):
    key = jax.random.fold_in(key, 11)
    rate_top = 1.0 / 30.0
    return decay_table(key, NLON, KV, rate_top)


def draw_lat_decay(key, part):
    key = jax.random.fold_in(key, 17)
    rate_top = 1.0 / 30.0
    return decay_table(key, NLAT, KV, rate_top)


def draw_increment(key, part):
    key = jax.random.fold_in(key, 23)
    noisy_component = jax.random.normal(key, (NLAT, NLON, KV), jnp.float32)
    return jnp.clip(noisy_component, -6.0, 6.0)


def block_levels(key, dims, cuts, smallest, largest):
    def one(position, shards_of):
        steps = jax.random.uniform(jax.random.fold_in(jax.random.fold_in(key, 6), position), (shards_of,), jnp.float32, smallest / len(cuts), largest / len(cuts))
        return jnp.repeat(jnp.exp(steps), dims[position] // shards_of).reshape((-1,) + (1,) * (len(dims) - position - 1))

    gain = one(*cuts[0])
    for cut in cuts[1:]:
        gain = gain * one(*cut)
    return gain


def gaussian(rng, extent, width, reach, kind=jnp.bfloat16):
    drawn = width * jax.random.normal(rng, extent, jnp.float32)
    return jnp.clip(drawn, min=-reach, max=reach).astype(kind)


def setup_inputs(seed: int = 0) -> dict:
    streams_of = jax.random.split(jax.random.key(seed), 6)
    increment = draw_increment(jax.random.fold_in(streams_of[5], 71), 0)
    error_std = jnp.clip(jnp.exp(math.log(3.0) - 2.3025851 * jax.random.uniform(streams_of[1], (NLAT, NLON, KV), jnp.float32) ** block_levels(streams_of[1], (NLAT, NLON, KV), ((0, 8), (1, 32)), -0.2, 0.2)), 0.3, 3.0)
    vertical = gaussian(streams_of[2], (NVAR, NLEV, NLEV), NLEV ** -0.5, 0.75, jnp.float32)
    lon_decay = draw_lon_decay(jax.random.fold_in(streams_of[5], 71), 0)
    lat_decay = draw_lat_decay(jax.random.fold_in(streams_of[5], 71), 0)
    return {"increment": increment, "error_std": error_std, "vertical": vertical, "lon_decay": lon_decay, "lat_decay": lat_decay}


PRECISE = lax.Precision.HIGHEST


def block_matrix(vertical):
    var_count = vertical.shape[0]
    lev_count = vertical.shape[1]
    selector = jnp.eye(var_count, dtype=vertical.dtype)
    expanded = vertical[:, :, None, :] * selector[:, None, :, None]
    return expanded.reshape(var_count * lev_count, var_count * lev_count)


def sweep_line(values, decays, periodic):
    def advance(carried, operands):
        current, factor = operands
        updated = factor[None, :] * carried + (1.0 - factor)[None, :] * current
        return updated, updated

    zero_state = jnp.zeros(values.shape[1:], jnp.float32)
    last_state, swept_line = lax.scan(advance, zero_state, (values, decays))
    if periodic:
        def product(carried, factor):
            updated = carried * factor
            return updated, updated

        loop_factor, growth = lax.scan(product, jnp.ones(decays.shape[1:], jnp.float32), decays)
        loop_state = last_state / (1.0 - loop_factor)[None, :]
        swept_line = swept_line + growth[:, None, :] * loop_state[None]
    return swept_line


def reference(increment, error_std, vertical, lon_decay, lat_decay):
    vert_block = block_matrix(vertical)
    working = jnp.einsum('abk,kl->abl', error_std * increment, vert_block, precision=PRECISE)
    column_list = jnp.swapaxes(working, 0, 1)
    for repeat in range(2):
        column_list = sweep_line(column_list, lon_decay, True)
        column_list = sweep_line(column_list[::-1], lon_decay[::-1], True)[::-1]
    working = jnp.swapaxes(column_list, 0, 1)
    for repeat in range(2):
        working = sweep_line(working, lat_decay, False)
        working = sweep_line(working[::-1], lat_decay[::-1], False)[::-1]
    return error_std * jnp.einsum('abl,kl->abk', working, vert_block, precision=PRECISE)
```

```python
import jax
import jax.numpy as jnp
from jax import lax
from jax.experimental import pallas as pl
from jax.experimental.pallas import tpu as pltpu
from jax.sharding import PartitionSpec as P

MESH = pl.DeviceIdType.MESH
F32 = jnp.float32
BF16 = jnp.bfloat16
NLAT, NLON, LANES = 64, 16, 128
ROWS = NLAT * NLON
CHIPS, LATS = 16, 8
HALF = range(2)
STATES = range(4)


def split(x):
    high = x.astype(BF16)
    return high, (x - high.astype(F32)).astype(BF16)


def dot3(x, high_ref, low_ref):
    high, low = split(x)
    dot = lambda a, b: jnp.dot(a, b, preferred_element_type=F32)
    return dot(high, high_ref[...]) + (dot(low, high_ref[...]) + dot(high, low_ref[...]))


def one_hot(k):
    return jnp.where(lax.broadcasted_iota(jnp.int32, (8, LANES), 0) == k, 1.0, 0.0).astype(F32)


def store_coefs(ref, at, base, ends):
    e1, e2, e3, e4 = ends
    for row, part in enumerate((e1[0:1], e2[0:1], e3[1:2], e3[0:1], e4[1:2], e4[0:1])):
        ref[(*at, pl.ds(base + row, 1), slice(None))] = part
    ref[(*at, pl.ds(base + 6, 2), slice(None))] = jnp.zeros((2, LANES), F32)


def kernel(
    inc, std, vert, lond, latd, out,
    inc_v, std_v, vert_v, lond_v, latd_v, out_v,
    vhi, vlo, thi, tlo, work, temp, lonu, latu, adj, xcol,
    pair_out, seg, segco, chipco, coin,
    s_out, s_in, x_out, x_in, unm, xlon,
    latz, latc, latx, latcx,
    lsem, osem, ssem, rsem,
):
    lon, lat = lax.axis_index("lon"), lax.axis_index("lat")
    core, chip = lax.rem(lon, 2), lon // 2
    other = 1 - core
    partner = {"lon": 2 * chip + other}
    chip_at = lambda k: lax.rem(chip + k, CHIPS)
    peer = lambda k: {"lon": 2 * chip_at(k) + core}
    lat_peer = lambda k: {"lat": lax.rem(lat + k, LATS)}

    barrier = pltpu.get_barrier_semaphore()
    pl.semaphore_signal(barrier, inc=1, device_id=partner, device_id_type=MESH)
    for k in range(1, CHIPS):
        pl.semaphore_signal(barrier, inc=1, device_id=peer(k), device_id_type=MESH)
    for k in range(1, LATS):
        pl.semaphore_signal(barrier, inc=1, device_id=lat_peer(k), device_id_type=MESH)

    loads = [pltpu.make_async_copy(a, b, lsem.at[i]) for i, (a, b) in enumerate(((lond, lond_v), (vert, vert_v), (latd, latd_v)))]
    for copy in loads:
        copy.start()
    parts = 4
    size = ROWS // parts
    big = []
    for i in range(parts):
        rows = pl.ds(i * size, size)
        big.append((
            pltpu.make_async_copy(inc.at[rows], inc_v.at[rows], lsem.at[3 + 2 * i]),
            pltpu.make_async_copy(std.at[rows], std_v.at[rows], lsem.at[4 + 2 * i]),
        ))
        for copy in big[-1]:
            copy.start()

    def send(src, dst, which, device):
        copy = pltpu.make_async_remote_copy(
            src_ref=src, dst_ref=dst, send_sem=ssem.at[which], recv_sem=rsem.at[which],
            device_id=device, device_id_type=MESH,
        )
        copy.start()

    def arrived(ref, which):
        pltpu.make_async_copy(ref, ref, rsem.at[which]).wait()

    def sent(ref, which):
        pltpu.make_async_copy(ref, ref, ssem.at[which]).wait()

    loads[0].wait()
    lanes = lambda h: pl.ds(h * LANES, LANES)
    lon_row = lambda i, h: lond_v[pl.ds(i, 1), lanes(h)]
    for h in HALF:
        ends = []
        line = [None] * NLON
        for k in STATES:
            y = one_hot(k)
            for i in range(NLON) if k % 2 == 0 else reversed(range(NLON)):
                d = lon_row(i, h)
                y = d * y if line[i] is None else d * y + (1.0 - d) * line[i]
                line[i] = y
            ends.append(y)
        for i in range(NLON):
            lonu[h, pl.ds(8 * i, 8), :] = line[i]
        store_coefs(segco, (core, h), 0, ends)

    loads[1].wait()
    vhi[...] = jnp.zeros_like(vhi)
    vlo[...] = jnp.zeros_like(vlo)
    thi[...] = jnp.zeros_like(thi)
    tlo[...] = jnp.zeros_like(tlo)
    zero64 = jnp.zeros((64, 64), F32)
    for p in range(2):
        a, b = vert_v[2 * p], vert_v[2 * p + 1]
        block = jnp.concatenate(
            [jnp.concatenate([a, zero64], axis=1), jnp.concatenate([zero64, b], axis=1)], axis=0
        )
        at = (pl.ds(p * LANES, LANES), pl.ds(p * LANES, LANES))
        vhi[at], vlo[at] = split(block)
        thi[at], tlo[at] = split(block.T)

    for i in range(parts):
        for copy in big[i]:
            copy.wait()
        rows = pl.ds(i * size, size)
        product = dot3(inc_v[rows, :] * std_v[rows, :], vhi, vlo)
        for h in HALF:
            work[h, rows, :] = product[:, h * LANES:(h + 1) * LANES]

    pl.semaphore_wait(barrier, CHIPS + LATS - 1)
    send(segco.at[core], segco.at[core], 0, partner)

    def lon_sweeps(half, put):
        first = half * (ROWS // 2)
        rows = lambda i: pl.ds(first + i, 32, stride=NLON)
        for k in STATES:
            ys = [jnp.zeros((32, LANES), F32)] * 2
            for i in range(NLON) if k % 2 == 0 else reversed(range(NLON)):
                for h in HALF:
                    u = work[h, rows(i), :] if k == 0 else temp[h, i]
                    d = lon_row(i, h)
                    ys[h] = d * ys[h] + (1.0 - d) * u
                    if k < 3:
                        temp[h, i] = ys[h]
                    else:
                        work[h, rows(i), :] = ys[h]
            for h in HALF:
                put(h, k, ys[h])

    def put_out(h, k, y):
        pair_out[h, k] = y

    def put_own(h, k, y):
        seg[core, h, k] = y

    lon_sweeps(other, put_out)
    send(pair_out, seg.at[core], 1, partner)

    arrived(segco.at[other], 0)
    co = lambda s, h, r: segco[s, h, pl.ds(r, 1), :]
    for h in HALF:
        g_l, a21_l, a32_l, a31_l, a42_l, a41_l = (co(0, h, r) for r in range(6))
        g_r, a21_r, a32_r, a31_r, a42_r, a41_r = (co(1, h, r) for r in range(6))
        b1 = a21_r * g_l
        f2 = a32_l * b1 + a31_l
        b2 = a21_r * f2 + a41_r * g_l
        f2b = a32_l * g_r
        values = (
            g_l * g_r,
            g_l * b1 + a21_l,
            g_r * f2b + a32_r,
            g_r * f2 + a31_r * g_l,
            g_l * (a21_r * f2b + a42_r) + a42_l * g_r,
            g_l * b2 + a42_l * b1 + a41_l,
        )
        for r, value in enumerate(values):
            chipco[h, pl.ds(r, 1), :] = value
        chipco[h, pl.ds(6, 2), :] = jnp.zeros((2, LANES), F32)
    coin[0] = chipco[chip // 8]
    for k in range(1, CHIPS):
        send(chipco.at[chip_at(k) // 8], coin.at[CHIPS - k], 2, peer(k))

    lon_sweeps(core, put_own)

    arrived(seg.at[other], 1)
    for h in HALF:
        g_l, a21_l, a32_l, a31_l, a42_l, a41_l = (co(0, h, r) for r in range(6))
        g_r, a21_r, a32_r, a31_r, a42_r, a41_r = (co(1, h, r) for r in range(6))
        l1, l2, l3, l4 = (seg[0, h, k] for k in STATES)
        r1, r2, r3, r4 = (seg[1, h, k] for k in STATES)
        b1 = a21_r * l1 + r2
        f2 = a32_l * b1 + l3
        b2 = a21_r * f2 + a41_r * l1 + r4
        merged = (
            g_r * l1 + r1,
            g_l * b1 + l2,
            g_r * f2 + a31_r * l1 + r3,
            g_l * b2 + a42_l * b1 + l4,
        )
        for k in STATES:
            for j in range(8):
                s_out[8 * h + j, k] = merged[k][4 * j:4 * j + 4]
    for k in range(1, CHIPS):
        send(s_out.at[chip_at(k)], s_in.at[CHIPS - k], 3, peer(k))
    s_in[0] = s_out[chip]

    loads[2].wait()
    latu[...] = jnp.zeros_like(latu)

    def lat_sweep(lines, reverse, carry):
        def body(step, ys):
            ys = list(ys)
            first = pl.multiple_of((NLAT // 8 - 1 - step if reverse else step) * 8, 8)
            decays = [latd_v[pl.ds(first, 8), lanes(h)] for h in HALF]
            for j in reversed(range(8)) if reverse else range(8):
                i = first + j
                for n, (ref, h, height) in enumerate(lines):
                    d = decays[h][j:j + 1]
                    at = pl.ds(pl.multiple_of(i * height, height), height)
                    ys[n] = d * ys[n] + (1.0 - d) * ref[h, at, :]
                    ref[h, at, :] = ys[n]
            return tuple(ys)

        return lax.fori_loop(0, NLAT // 8, body, tuple(carry))

    lines = [(work, 0, 16), (work, 1, 16), (latu, 0, 8), (latu, 1, 8)]
    ends = []
    for k in STATES:
        start = [jnp.zeros((16, LANES), F32)] * 2 + [one_hot(k)] * 2
        ends.append(lat_sweep(lines, k % 2 == 1, start))
    for h in HALF:
        for k in STATES:
            latz[lat, h, pl.ds(16 * k, 16), :] = ends[k][h]
        store_coefs(latz, (lat, h), 64, [e[2 + h] for e in ends])
    for k in range(1, LATS):
        send(latz.at[lat], latz.at[lat], 4, lat_peer(k))

    arrived(coin.at[pl.ds(1, CHIPS - 1)], 2)
    cc = [[coin[j, pl.ds(r, 1), :] for r in range(6)] for j in range(CHIPS)]
    ahead, behind = [jnp.ones((1, LANES), F32)], [jnp.ones((1, LANES), F32)]
    for j in range(CHIPS):
        ahead.append(ahead[-1] * cc[j][0])
        behind.append(behind[-1] * cc[CHIPS - 1 - j][0])
    close = 1.0 / (1.0 - ahead[CHIPS])
    arrived(s_in.at[pl.ds(1, CHIPS - 1)], 3)

    def ring(terms, reverse):
        t = jnp.zeros((4, LANES), F32)
        before = [None] * CHIPS
        order = range(CHIPS - 1, -1, -1) if reverse else range(CHIPS)
        for j in order:
            before[j] = t
            t = cc[j][0] * t + terms[j]
        start = t * close
        growth = (lambda j: behind[CHIPS - 1 - j]) if reverse else (lambda j: ahead[j])
        return [before[j] + growth(j) * start for j in range(CHIPS)]

    seat = range(CHIPS)
    x1 = ring([s_in[j, 0] for j in seat], False)
    x2 = ring([s_in[j, 1] + cc[j][1] * x1[j] for j in seat], True)
    x3 = ring([s_in[j, 2] + cc[j][3] * x1[j] + cc[j][2] * x2[j] for j in seat], False)
    x4 = ring([s_in[j, 3] + cc[j][5] * x1[j] + cc[j][4] * x2[j] + cc[j][1] * x3[j] for j in seat], True)
    for j in seat:
        for k, x in enumerate((x1, x2, x3, x4)):
            x_out[j, k] = x[j]
    for k in range(1, CHIPS):
        send(x_out.at[k], x_in.at[chip], 5, peer(k))
    x_in[chip] = x_out[0]

    adj[...] = jnp.zeros_like(adj)

    def adjoint(reverse, carry):
        def body(step, cs):
            cs = list(cs)
            first = pl.multiple_of((NLAT // 8 - 1 - step if reverse else step) * 8, 8)
            decays = [latd_v[pl.ds(first, 8), lanes(h)] for h in HALF]
            for j in reversed(range(8)) if reverse else range(8):
                at = pl.ds(pl.multiple_of((first + j) * 8, 8), 8)
                for h in HALF:
                    d = decays[h][j:j + 1]
                    t = adj[h, at, :] + cs[h]
                    adj[h, at, :] = (1.0 - d) * t
                    cs[h] = d * t
            return tuple(cs)

        lax.fori_loop(0, NLAT // 8, body, tuple(carry))

    for k in (3, 2, 1, 0):
        adjoint(k % 2 == 0, [one_hot(k)] * 2)

    def lat_solve(state, coef, put, zero):
        x1, x2, x3, x4 = ([zero] * LATS for _ in STATES)
        for p in range(LATS - 1):
            x1[p + 1] = coef(p, 0) * x1[p] + state(p, 0)
        for p in range(LATS - 1, 0, -1):
            x2[p - 1] = coef(p, 0) * x2[p] + (coef(p, 1) * x1[p] + state(p, 1))
        for p in range(LATS - 1):
            x3[p + 1] = coef(p, 0) * x3[p] + (coef(p, 2) * x2[p] + coef(p, 3) * x1[p] + state(p, 2))
        for p in range(LATS - 1, 0, -1):
            x4[p - 1] = coef(p, 0) * x4[p] + (
                coef(p, 1) * x3[p] + coef(p, 4) * x2[p] + coef(p, 5) * x1[p] + state(p, 3)
            )
        for p in range(LATS):
            for k, x in enumerate((x1, x2, x3, x4)):
                put(p, k, x[p])

    arrived(latz.at[pl.ds(0, LATS - 1)], 4)
    for h in HALF:
        def put_z(p, k, x, h=h):
            latx[p, h, pl.ds(16 * k, 16), :] = x

        lat_solve(
            lambda p, k: latz[p, h, pl.ds(16 * k, 16), :],
            lambda p, r: latz[p, h, pl.ds(64 + r, 1), :],
            put_z, jnp.zeros((16, LANES), F32),
        )

    arrived(x_in.at[pl.ds(0, CHIPS - 1)], 5)
    for h in HALF:
        g_l, a21_l, a32_l, a31_l, a42_l, a41_l = (co(0, h, r) for r in range(6))
        g_r, a21_r, a32_r, a31_r, a42_r, a41_r = (co(1, h, r) for r in range(6))
        l1, l2, l3, l4 = (seg[0, h, k] for k in STATES)
        r1, r2, r3, r4 = (seg[1, h, k] for k in STATES)
        e1, e2, e3, e4 = (jnp.concatenate([x_in[8 * h + j, k] for j in range(8)], axis=0) for k in STATES)
        f1 = g_l * e1 + l1
        b1 = g_r * e2 + a21_r * f1 + r2
        f2 = g_l * e3 + a32_l * b1 + a31_l * e1 + l3
        b2 = g_r * e4 + a21_r * f2 + a42_r * e2 + a41_r * f1 + r4
        for k, (left, right) in enumerate(((e1, f1), (b1, e2), (e3, f2), (b2, e4))):
            unm[0, h, k] = left
            unm[1, h, k] = right
    send(unm.at[other], xlon.at[core], 6, partner)
    xlon[core] = unm[core]
    xcol[...] = jnp.zeros_like(xcol)
    arrived(xlon.at[other], 6)

    for h in HALF:
        for k in STATES:
            weights = adj[h, pl.ds(k, NLAT, stride=8), :]
            for c in STATES:
                total = weights[0:32] * xlon[0, h, c] + weights[32:64] * xlon[1, h, c]
                latc[lat, h, pl.ds(4 * k + c, 1), :] = jnp.sum(total, axis=0, keepdims=True)
    for k in range(1, LATS):
        send(latc.at[lat], latc.at[lat], 7, lat_peer(k))

    for h in HALF:
        for half in range(2):
            for c in STATES:
                xcol[h, pl.ds(256 * half + c, 32, stride=8), :] = xlon[half, h, c]
    lines = [(xcol, 0, 8), (xcol, 1, 8)]
    for k in STATES:
        lat_sweep(lines, k % 2 == 1, [jnp.zeros((8, LANES), F32)] * 2)
    lon_unit = [[lonu[h, pl.ds(c, NLON, stride=8), :] for c in STATES] for h in HALF]

    def add_lon(step, _):
        for j in range(4):
            i = step * 4 + j
            for h in HALF:
                at = pl.ds(pl.multiple_of(i * 16, 16), 16)
                y = work[h, at, :]
                column = xcol[h, pl.ds(pl.multiple_of(i * 8, 8), 8), :]
                for c in STATES:
                    y = y + column[c:c + 1] * lon_unit[h][c]
                work[h, at, :] = y
        return 0

    lax.fori_loop(0, NLAT // 4, add_lon, 0)

    arrived(latc.at[pl.ds(0, LATS - 1)], 7)
    enter = []
    for h in HALF:
        def put_c(p, k, x, h=h):
            latcx[p, h, pl.ds(4 * k, 4), :] = x

        lat_solve(
            lambda p, k: latc[p, h, pl.ds(4 * k, 4), :],
            lambda p, r: latz[p, h, pl.ds(64 + r, 1), :],
            put_c, jnp.zeros((4, LANES), F32),
        )
        for k in STATES:
            x = latx[lat, h, pl.ds(16 * k, 16), :]
            for c in STATES:
                x = x + lon_unit[h][c] * latcx[lat, h, pl.ds(4 * k + c, 1), :]
            enter.append(x)

    def finish(step, _):
        for h in HALF:
            for j in range(8):
                i = step * 8 + j
                at = pl.ds(pl.multiple_of(i * 16, 16), 16)
                y = work[h, at, :]
                unit = latu[h, pl.ds(pl.multiple_of(i * 8, 8), 8), :]
                for k in STATES:
                    y = y + unit[k:k + 1] * enter[4 * h + k]
                inc_v[at, lanes(h)] = y
        rows = pl.ds(pl.multiple_of(step * 128, 128), 128)
        out_v[rows, :] = std_v[rows, :] * dot3(inc_v[rows, :], thi, tlo)
        pltpu.make_async_copy(out_v.at[rows], out.at[rows], osem.at[0]).start()
        return 0

    lax.fori_loop(0, 8, finish, 0)
    pltpu.make_async_copy(out_v, out, osem.at[0]).wait()
    sent(segco.at[core], 0)
    sent(pair_out, 1)
    sent(coin.at[pl.ds(1, CHIPS - 1)], 2)
    sent(s_in.at[pl.ds(1, CHIPS - 1)], 3)
    sent(latz.at[pl.ds(0, LATS - 1)], 4)
    sent(x_in.at[pl.ds(0, CHIPS - 1)], 5)
    sent(unm.at[other], 6)
    sent(latc.at[pl.ds(0, LATS - 1)], 7)


def per_device(increment, error_std, vertical, lon_decay, lat_decay):
    vmem = lambda *shape: pltpu.VMEM(shape, F32)
    result = pl.pallas_call(
        kernel,
        out_shape=jax.ShapeDtypeStruct((ROWS, 256), F32),
        in_specs=[pl.BlockSpec(memory_space=pl.ANY)] * 5,
        out_specs=pl.BlockSpec(memory_space=pl.ANY),
        scratch_shapes=[
            vmem(ROWS, 256), vmem(ROWS, 256), vmem(4, 64, 64), vmem(NLON, 256), vmem(NLAT, 256), vmem(ROWS, 256),
            *[pltpu.VMEM((256, 256), BF16)] * 4,
            vmem(2, ROWS, LANES), vmem(2, NLON, 32, LANES), vmem(2, NLON * 8, LANES),
            *[vmem(2, NLAT * 8, LANES)] * 3,
            vmem(2, 4, 32, LANES), vmem(2, 2, 4, 32, LANES), vmem(2, 2, 8, LANES), vmem(2, 8, LANES), vmem(CHIPS, 8, LANES),
            *[vmem(CHIPS, 4, 4, LANES)] * 4,
            vmem(2, 2, 4, 32, LANES), vmem(2, 2, 4, 32, LANES),
            vmem(LATS, 2, 72, LANES), vmem(LATS, 2, 16, LANES), vmem(LATS, 2, 64, LANES), vmem(LATS, 2, 16, LANES),
            pltpu.SemaphoreType.DMA((11,)), pltpu.SemaphoreType.DMA((1,)),
            pltpu.SemaphoreType.DMA((8,)), pltpu.SemaphoreType.DMA((8,)),
        ],
        compiler_params=pltpu.CompilerParams(
            collective_id=0, has_side_effects=True, vmem_limit_bytes=24 * 1024 * 1024
        ),
    )(*[
        pltpu.with_memory_space_constraint(x, pltpu.HBM)
        for x in (increment.reshape(ROWS, 256), error_std.reshape(ROWS, 256), vertical, lon_decay, lat_decay)
    ])
    return result.reshape(NLAT, NLON, 256)


def solution(mesh):
    placed = (P("lat", "lon", None), P("lat", "lon", None), P(), P("lon", None), P("lat", None))
    return jax.shard_map(
        per_device, mesh=mesh, in_specs=placed, out_specs=P("lat", "lon", None), check_vma=False
    )
```

```python
import jax
import jax.numpy as jnp
from jax import lax
from jax.experimental import pallas as pl
from jax.experimental.pallas import tpu as pltpu
from jax.sharding import PartitionSpec as P

MESH = pl.DeviceIdType.MESH
F32 = jnp.float32
BF16 = jnp.bfloat16
NLAT, NLON, LANES = 64, 16, 128
ROWS = NLAT * NLON
CHIPS, LATS = 16, 8
FAR_CHIPS = sorted(range(1, CHIPS), key=lambda k: -min(k, CHIPS - k))
FAR_LATS = sorted(range(1, LATS), key=lambda k: -min(k, LATS - k))
HALF = range(2)
STATES = range(4)


def split(x):
    high = x.astype(BF16)
    return high, (x - high.astype(F32)).astype(BF16)


def dot3(x, high_ref, low_ref):
    high, low = split(x)
    dot = lambda a, b: jnp.dot(a, b, preferred_element_type=F32)
    rows = x.shape[0]
    both = dot(jnp.concatenate([high, low], axis=0), high_ref[...])
    return both[:rows] + (both[rows:] + dot(high, low_ref[...]))


def one_hot(k):
    return jnp.where(lax.broadcasted_iota(jnp.int32, (8, LANES), 0) == k, 1.0, 0.0).astype(F32)


def store_coefs(ref, at, base, ends):
    e1, e2, e3, e4 = ends
    for row, part in enumerate((e1[0:1], e2[0:1], e3[1:2], e3[0:1], e4[1:2], e4[0:1])):
        ref[(*at, pl.ds(base + row, 1), slice(None))] = part
    ref[(*at, pl.ds(base + 6, 2), slice(None))] = jnp.zeros((2, LANES), F32)


def kernel(
    inc, std, vert, lond, latd,
    work, latu, enter, std_v, thi, tlo,
    inc_v, vert_v, lond_v, latd_v,
    vhi, vlo, temp, lonu, adj, xcol,
    pair_out, seg, segco, chipco, coin,
    s_out, s_in, x_out, x_in, unm, xlon,
    latz, latc, lato, latx, latcx,
    lsem, ssem, rsem,
):
    lon, lat = lax.axis_index("lon"), lax.axis_index("lat")
    core, chip = lax.rem(lon, 2), lon // 2
    other = 1 - core
    partner = {"lon": 2 * chip + other}
    chip_at = lambda k: lax.rem(chip + k, CHIPS)
    peer = lambda k: {"lon": 2 * chip_at(k) + core}
    lat_peer = lambda k: {"lat": lax.rem(lat + k, LATS)}
    cross_peer = lambda k: {"lon": 2 * chip + other, "lat": lax.rem(lat + k, LATS)}

    barrier = pltpu.get_barrier_semaphore()
    greeted = [peer(k) for k in FAR_CHIPS] + [p(k) for k in FAR_LATS for p in (lat_peer, cross_peer)] + [partner]
    for device in greeted:
        pl.semaphore_signal(barrier, inc=1, device_id=device, device_id_type=MESH)

    loads = [pltpu.make_async_copy(a, b, lsem.at[i]) for i, (a, b) in enumerate(((lond, lond_v), (vert, vert_v), (latd, latd_v)))]
    for copy in loads:
        copy.start()
    parts = 4
    size = ROWS // parts
    big = []
    for i in range(parts):
        rows = pl.ds(i * size, size)
        big.append((
            pltpu.make_async_copy(inc.at[rows], inc_v.at[rows], lsem.at[3 + 2 * i]),
            pltpu.make_async_copy(std.at[rows], std_v.at[rows], lsem.at[4 + 2 * i]),
        ))
        for copy in big[-1]:
            copy.start()

    def send(src, dst, which, device):
        copy = pltpu.make_async_remote_copy(
            src_ref=src, dst_ref=dst, send_sem=ssem.at[which], recv_sem=rsem.at[which],
            device_id=device, device_id_type=MESH,
        )
        copy.start()

    def arrived(ref, which):
        pltpu.make_async_copy(ref, ref, rsem.at[which]).wait()

    def sent(ref, which):
        pltpu.make_async_copy(ref, ref, ssem.at[which]).wait()

    loads[0].wait()
    lanes = lambda h: pl.ds(h * LANES, LANES)
    lon_row = lambda i, h: lond_v[pl.ds(i, 1), lanes(h)]
    for h in HALF:
        ends = []
        line = [None] * NLON
        for k in STATES:
            y = one_hot(k)
            for i in range(NLON) if k % 2 == 0 else reversed(range(NLON)):
                d = lon_row(i, h)
                y = d * y if line[i] is None else d * y + (1.0 - d) * line[i]
                line[i] = y
            ends.append(y)
        for i in range(NLON):
            lonu[h, pl.ds(8 * i, 8), :] = line[i]
        store_coefs(segco, (core, h), 0, ends)

    loads[1].wait()
    vhi[...] = jnp.zeros_like(vhi)
    vlo[...] = jnp.zeros_like(vlo)
    thi[...] = jnp.zeros_like(thi)
    tlo[...] = jnp.zeros_like(tlo)
    zero64 = jnp.zeros((64, 64), F32)
    for p in range(2):
        a, b = vert_v[2 * p], vert_v[2 * p + 1]
        block = jnp.concatenate(
            [jnp.concatenate([a, zero64], axis=1), jnp.concatenate([zero64, b], axis=1)], axis=0
        )
        at = (pl.ds(p * LANES, LANES), pl.ds(p * LANES, LANES))
        vhi[at], vlo[at] = split(block)
        thi[at], tlo[at] = split(block.T)

    for i in range(parts):
        for copy in big[i]:
            copy.wait()
        rows = pl.ds(i * size, size)
        product = dot3(inc_v[rows, :] * std_v[rows, :], vhi, vlo)
        for h in HALF:
            work[h, rows, :] = product[:, h * LANES:(h + 1) * LANES]

    def lon_sweeps(half, put):
        first = half * (ROWS // 2)
        rows = lambda i: pl.ds(first + i, 32, stride=NLON)
        for k in STATES:
            ys = [jnp.zeros((32, LANES), F32)] * 2
            for i in range(NLON) if k % 2 == 0 else reversed(range(NLON)):
                for h in HALF:
                    u = work[h, rows(i), :] if k == 0 else temp[h, i]
                    d = lon_row(i, h)
                    ys[h] = d * ys[h] + (1.0 - d) * u
                    if k < 3:
                        temp[h, i] = ys[h]
                    else:
                        work[h, rows(i), :] = ys[h]
            for h in HALF:
                put(h, k, ys[h])

    def put_out(h, k, y):
        pair_out[h, k] = y

    def put_own(h, k, y):
        seg[core, h, k] = y

    lon_sweeps(other, put_out)
    pl.semaphore_wait(barrier, len(greeted))
    send(segco.at[core], segco.at[core], 0, partner)
    send(pair_out, seg.at[core], 1, partner)

    arrived(segco.at[other], 0)
    co = lambda s, h, r: segco[s, h, pl.ds(r, 1), :]
    for h in HALF:
        g_l, a21_l, a32_l, a31_l, a42_l, a41_l = (co(0, h, r) for r in range(6))
        g_r, a21_r, a32_r, a31_r, a42_r, a41_r = (co(1, h, r) for r in range(6))
        b1 = a21_r * g_l
        f2 = a32_l * b1 + a31_l
        b2 = a21_r * f2 + a41_r * g_l
        f2b = a32_l * g_r
        values = (
            g_l * g_r,
            g_l * b1 + a21_l,
            g_r * f2b + a32_r,
            g_r * f2 + a31_r * g_l,
            g_l * (a21_r * f2b + a42_r) + a42_l * g_r,
            g_l * b2 + a42_l * b1 + a41_l,
        )
        for r, value in enumerate(values):
            chipco[h, pl.ds(r, 1), :] = value
        chipco[h, pl.ds(6, 2), :] = jnp.zeros((2, LANES), F32)
    coin[0] = chipco[chip // 8]
    for k in FAR_CHIPS:
        send(chipco.at[chip_at(k) // 8], coin.at[CHIPS - k], 2, peer(k))

    lon_sweeps(core, put_own)

    arrived(seg.at[other], 1)
    for h in HALF:
        g_l, a21_l, a32_l, a31_l, a42_l, a41_l = (co(0, h, r) for r in range(6))
        g_r, a21_r, a32_r, a31_r, a42_r, a41_r = (co(1, h, r) for r in range(6))
        l1, l2, l3, l4 = (seg[0, h, k] for k in STATES)
        r1, r2, r3, r4 = (seg[1, h, k] for k in STATES)
        b1 = a21_r * l1 + r2
        f2 = a32_l * b1 + l3
        b2 = a21_r * f2 + a41_r * l1 + r4
        merged = (
            g_r * l1 + r1,
            g_l * b1 + l2,
            g_r * f2 + a31_r * l1 + r3,
            g_l * b2 + a42_l * b1 + l4,
        )
        for k in STATES:
            for j in range(8):
                s_out[8 * h + j, k] = merged[k][4 * j:4 * j + 4]
    for k in FAR_CHIPS:
        send(s_out.at[chip_at(k)], s_in.at[CHIPS - k], 3, peer(k))
    s_in[0] = s_out[chip]

    loads[2].wait()
    latu[...] = jnp.zeros_like(latu)

    def lat_sweep(lines, reverse, carry):
        def body(step, ys):
            ys = list(ys)
            first = pl.multiple_of((NLAT // 8 - 1 - step if reverse else step) * 8, 8)
            decays = [latd_v[pl.ds(first, 8), lanes(h)] for h in HALF]
            for j in reversed(range(8)) if reverse else range(8):
                i = first + j
                for n, (ref, h, height) in enumerate(lines):
                    d = decays[h][j:j + 1]
                    at = pl.ds(pl.multiple_of(i * height, height), height)
                    ys[n] = d * ys[n] + (1.0 - d) * ref[h, at, :]
                    ref[h, at, :] = ys[n]
            return tuple(ys)

        return lax.fori_loop(0, NLAT // 8, body, tuple(carry))

    lines = [(work, 0, 16), (work, 1, 16), (latu, 0, 8), (latu, 1, 8)]
    ends = []
    for k in STATES:
        start = [jnp.zeros((16, LANES), F32)] * 2 + [one_hot(k)] * 2
        ends.append(lat_sweep(lines, k % 2 == 1, start))
    for h in HALF:
        for k in STATES:
            latz[lat, h, pl.ds(16 * k, 16), :] = ends[k][h]
        store_coefs(latz, (lat, h), 64, [e[2 + h] for e in ends])
    for k in FAR_LATS:
        send(latz.at[lat], latz.at[lat], 4, lat_peer(k))

    arrived(coin.at[pl.ds(1, CHIPS - 1)], 2)
    cc = [[coin[j, pl.ds(r, 1), :] for r in range(6)] for j in range(CHIPS)]
    ahead, behind = [jnp.ones((1, LANES), F32)], [jnp.ones((1, LANES), F32)]
    for j in range(CHIPS):
        ahead.append(ahead[-1] * cc[j][0])
        behind.append(behind[-1] * cc[CHIPS - 1 - j][0])
    close = 1.0 / (1.0 - ahead[CHIPS])
    arrived(s_in.at[pl.ds(1, CHIPS - 1)], 3)

    def ring(terms, reverse):
        t = jnp.zeros((4, LANES), F32)
        before = [None] * CHIPS
        order = range(CHIPS - 1, -1, -1) if reverse else range(CHIPS)
        for j in order:
            before[j] = t
            t = cc[j][0] * t + terms[j]
        start = t * close
        growth = (lambda j: behind[CHIPS - 1 - j]) if reverse else (lambda j: ahead[j])
        return [before[j] + growth(j) * start for j in range(CHIPS)]

    seat = range(CHIPS)
    x1 = ring([s_in[j, 0] for j in seat], False)
    x2 = ring([s_in[j, 1] + cc[j][1] * x1[j] for j in seat], True)
    x3 = ring([s_in[j, 2] + cc[j][3] * x1[j] + cc[j][2] * x2[j] for j in seat], False)
    x4 = ring([s_in[j, 3] + cc[j][5] * x1[j] + cc[j][4] * x2[j] + cc[j][1] * x3[j] for j in seat], True)
    for j in seat:
        for k, x in enumerate((x1, x2, x3, x4)):
            x_out[j, k] = x[j]
    for k in FAR_CHIPS:
        send(x_out.at[k], x_in.at[chip], 5, peer(k))
    x_in[chip] = x_out[0]

    adj[...] = jnp.zeros_like(adj)

    def adjoint(reverse, carry):
        def body(step, cs):
            cs = list(cs)
            first = pl.multiple_of((NLAT // 8 - 1 - step if reverse else step) * 8, 8)
            decays = [latd_v[pl.ds(first, 8), lanes(h)] for h in HALF]
            for j in reversed(range(8)) if reverse else range(8):
                at = pl.ds(pl.multiple_of((first + j) * 8, 8), 8)
                for h in HALF:
                    d = decays[h][j:j + 1]
                    t = adj[h, at, :] + cs[h]
                    adj[h, at, :] = (1.0 - d) * t
                    cs[h] = d * t
            return tuple(cs)

        lax.fori_loop(0, NLAT // 8, body, tuple(carry))

    for k in (3, 2, 1, 0):
        adjoint(k % 2 == 0, [one_hot(k)] * 2)

    def lat_solve(state, coef, put, zero):
        x1, x2, x3, x4 = ([zero] * LATS for _ in STATES)
        for p in range(LATS - 1):
            x1[p + 1] = coef(p, 0) * x1[p] + state(p, 0)
        for p in range(LATS - 1, 0, -1):
            x2[p - 1] = coef(p, 0) * x2[p] + (coef(p, 1) * x1[p] + state(p, 1))
        for p in range(LATS - 1):
            x3[p + 1] = coef(p, 0) * x3[p] + (coef(p, 2) * x2[p] + coef(p, 3) * x1[p] + state(p, 2))
        for p in range(LATS - 1, 0, -1):
            x4[p - 1] = coef(p, 0) * x4[p] + (
                coef(p, 1) * x3[p] + coef(p, 4) * x2[p] + coef(p, 5) * x1[p] + state(p, 3)
            )
        for p in range(LATS):
            for k, x in enumerate((x1, x2, x3, x4)):
                put(p, k, x[p])

    arrived(latz.at[pl.ds(0, LATS - 1)], 4)
    for h in HALF:
        def put_z(p, k, x, h=h):
            latx[p, h, pl.ds(16 * k, 16), :] = x

        lat_solve(
            lambda p, k: latz[p, h, pl.ds(16 * k, 16), :],
            lambda p, r: latz[p, h, pl.ds(64 + r, 1), :],
            put_z, jnp.zeros((16, LANES), F32),
        )

    arrived(x_in.at[pl.ds(0, CHIPS - 1)], 5)
    for h in HALF:
        g_l, a21_l, a32_l, a31_l, a42_l, a41_l = (co(0, h, r) for r in range(6))
        g_r, a21_r, a32_r, a31_r, a42_r, a41_r = (co(1, h, r) for r in range(6))
        l1, l2, l3, l4 = (seg[0, h, k] for k in STATES)
        r1, r2, r3, r4 = (seg[1, h, k] for k in STATES)
        e1, e2, e3, e4 = (jnp.concatenate([x_in[8 * h + j, k] for j in range(8)], axis=0) for k in STATES)
        f1 = g_l * e1 + l1
        b1 = g_r * e2 + a21_r * f1 + r2
        f2 = g_l * e3 + a32_l * b1 + a31_l * e1 + l3
        b2 = g_r * e4 + a21_r * f2 + a42_r * e2 + a41_r * f1 + r4
        for k, (left, right) in enumerate(((e1, f1), (b1, e2), (e3, f2), (b2, e4))):
            unm[0, h, k] = left
            unm[1, h, k] = right
    send(unm.at[other], xlon.at[core], 6, partner)

    weights = [[adj[h, pl.ds(256 * core + k, 32, stride=8), :] for k in STATES] for h in HALF]
    for whose, put in ((other, lambda h, r: lato.at[h, pl.ds(r, 1)]), (core, lambda h, r: latc.at[2 * lat + core, h, pl.ds(r, 1)])):
        for h in HALF:
            for c in STATES:
                x = unm[whose, h, c]
                for k in STATES:
                    put(h, 4 * k + c)[...] = jnp.sum(weights[h][k] * x, axis=0, keepdims=True)
        for k in FAR_LATS:
            if whose is other:
                send(lato, latc.at[2 * lat + core], 7, cross_peer(k))
            else:
                send(latc.at[2 * lat + core], latc.at[2 * lat + core], 7, lat_peer(k))
    send(lato, latc.at[2 * lat + core], 7, partner)

    xlon[core] = unm[core]
    xcol[...] = jnp.zeros_like(xcol)
    arrived(xlon.at[other], 6)
    for h in HALF:
        for half in range(2):
            for c in STATES:
                xcol[h, pl.ds(256 * half + c, 32, stride=8), :] = xlon[half, h, c]
    lines = [(xcol, 0, 8), (xcol, 1, 8)]
    for k in STATES:
        lat_sweep(lines, k % 2 == 1, [jnp.zeros((8, LANES), F32)] * 2)
    lon_unit = [[lonu[h, pl.ds(c, NLON, stride=8), :] for c in STATES] for h in HALF]

    def add_lon(step, _):
        for j in range(4):
            i = step * 4 + j
            for h in HALF:
                at = pl.ds(pl.multiple_of(i * 16, 16), 16)
                y = work[h, at, :]
                column = xcol[h, pl.ds(pl.multiple_of(i * 8, 8), 8), :]
                for c in STATES:
                    y = y + column[c:c + 1] * lon_unit[h][c]
                work[h, at, :] = y
        return 0

    lax.fori_loop(0, NLAT // 4, add_lon, 0)

    arrived(latc.at[pl.ds(0, 2 * LATS - 1)], 7)
    for h in HALF:
        def put_c(p, k, x, h=h):
            latcx[p, h, pl.ds(4 * k, 4), :] = x

        lat_solve(
            lambda p, k: latc[2 * p, h, pl.ds(4 * k, 4), :] + latc[2 * p + 1, h, pl.ds(4 * k, 4), :],
            lambda p, r: latz[p, h, pl.ds(64 + r, 1), :],
            put_c, jnp.zeros((4, LANES), F32),
        )
        for k in STATES:
            x = latx[lat, h, pl.ds(16 * k, 16), :]
            for c in STATES:
                x = x + lon_unit[h][c] * latcx[lat, h, pl.ds(4 * k + c, 1), :]
            enter[h, k] = x

    sent(segco.at[core], 0)
    sent(pair_out, 1)
    sent(coin.at[pl.ds(1, CHIPS - 1)], 2)
    sent(s_in.at[pl.ds(1, CHIPS - 1)], 3)
    sent(latz.at[pl.ds(0, LATS - 1)], 4)
    sent(x_in.at[pl.ds(0, CHIPS - 1)], 5)
    sent(unm.at[other], 6)
    sent(latc.at[pl.ds(0, 2 * LATS - 1)], 7)


def finish(work, latu, enter, std, thi, tlo, out, line, out_v, sem):
    parts = 4
    size = ROWS // parts

    def part(step, _):
        for h in HALF:
            for j in range(size // 16):
                i = step * (size // 16) + j
                y = work[h, pl.ds(pl.multiple_of(i * 16, 16), 16), :]
                unit = latu[h, pl.ds(pl.multiple_of(i * 8, 8), 8), :]
                for k in STATES:
                    y = y + unit[k:k + 1] * enter[h, k]
                line[pl.ds(16 * j, 16), pl.ds(h * LANES, LANES)] = y
        rows = pl.ds(pl.multiple_of(step * size, size), size)
        out_v[rows, :] = std[rows, :] * dot3(line[...], thi, tlo)
        pltpu.make_async_copy(out_v.at[rows], out.at[rows], sem.at[0]).start()
        return 0

    lax.fori_loop(0, parts, part, 0)
    pltpu.make_async_copy(out_v, out, sem.at[0]).wait()


def per_device(increment, error_std, vertical, lon_decay, lat_decay):
    vmem = lambda *shape: pltpu.VMEM(shape, F32)
    whole = pl.BlockSpec(memory_space=pltpu.VMEM)
    square = pltpu.VMEM((256, 256), BF16)
    held = pl.pallas_call(
        kernel,
        out_shape=[
            vmem(2, ROWS, LANES), vmem(2, NLAT * 8, LANES), vmem(2, 4, NLON, LANES), vmem(ROWS, 256), square, square,
        ],
        in_specs=[pl.BlockSpec(memory_space=pl.ANY)] * 5,
        out_specs=[whole] * 6,
        scratch_shapes=[
            vmem(ROWS, 256), vmem(4, 64, 64), vmem(NLON, 256), vmem(NLAT, 256),
            square, square, vmem(2, NLON, 32, LANES), vmem(2, NLON * 8, LANES),
            *[vmem(2, NLAT * 8, LANES)] * 2,
            vmem(2, 4, 32, LANES), vmem(2, 2, 4, 32, LANES), vmem(2, 2, 8, LANES), vmem(2, 8, LANES), vmem(CHIPS, 8, LANES),
            *[vmem(CHIPS, 4, 4, LANES)] * 4,
            vmem(2, 2, 4, 32, LANES), vmem(2, 2, 4, 32, LANES),
            vmem(LATS, 2, 72, LANES), vmem(2 * LATS, 2, 16, LANES), vmem(2, 16, LANES),
            vmem(LATS, 2, 64, LANES), vmem(LATS, 2, 16, LANES),
            pltpu.SemaphoreType.DMA((11,)), pltpu.SemaphoreType.DMA((8,)), pltpu.SemaphoreType.DMA((8,)),
        ],
        compiler_params=pltpu.CompilerParams(
            collective_id=0, has_side_effects=True, vmem_limit_bytes=24 * 1024 * 1024
        ),
    )(*[
        pltpu.with_memory_space_constraint(x, pltpu.HBM)
        for x in (increment.reshape(ROWS, 256), error_std.reshape(ROWS, 256), vertical, lon_decay, lat_decay)
    ])
    result = pl.pallas_call(
        finish,
        out_shape=jax.ShapeDtypeStruct((ROWS, 256), F32),
        in_specs=[whole] * 6,
        out_specs=pl.BlockSpec(memory_space=pl.ANY),
        scratch_shapes=[vmem(256, 256), vmem(ROWS, 256), pltpu.SemaphoreType.DMA((1,))],
        compiler_params=pltpu.CompilerParams(vmem_limit_bytes=24 * 1024 * 1024),
    )(*held)
    return result.reshape(NLAT, NLON, 256)


def solution(mesh):
    placed = (P("lat", "lon", None), P("lat", "lon", None), P(), P("lon", None), P("lat", None))
    return jax.shard_map(
        per_device, mesh=mesh, in_specs=placed, out_specs=P("lat", "lon", None), check_vma=False
    )
```

```python
import jax
import jax.numpy as jnp
from jax import lax
from jax.experimental import pallas as pl
from jax.experimental.pallas import tpu as pltpu
from jax.sharding import PartitionSpec as P

MESH = pl.DeviceIdType.MESH
F32 = jnp.float32
BF16 = jnp.bfloat16
NLAT, NLON, LANES = 64, 16, 128
ROWS = NLAT * NLON
LONS, CHIPS, LATS = 32, 16, 8
FAR_CHIPS = sorted(range(1, CHIPS), key=lambda k: -min(k, CHIPS - k))
FAR_LONS = sorted(range(1, LONS), key=lambda k: -min(k, LONS - k))
FAR_LATS = sorted(range(1, LATS), key=lambda k: -min(k, LATS - k))
HALF = range(2)
STATES = range(4)


def split(x):
    high = x.astype(BF16)
    return high, (x - high.astype(F32)).astype(BF16)


def dot3(x, weight):
    both = jnp.dot(jnp.concatenate(split(x), axis=1), weight, preferred_element_type=F32)
    return both[:, :LANES] + both[:, LANES:]


def one_hot(k):
    return jnp.where(lax.broadcasted_iota(jnp.int32, (8, LANES), 0) == k, 1.0, 0.0).astype(F32)


def store_coefs(ref, at, base, rows):
    for row, part in enumerate(rows):
        ref[(*at, pl.ds(base + row, 1), slice(None))] = part
    ref[(*at, pl.ds(base + 6, 2), slice(None))] = jnp.zeros((2, LANES), F32)


def kernel(
    inc, std, vert, lond, latd,
    work, latu, enter, std_v, tw,
    inc_v, vert_v, lond_v, latd_v,
    vw, temp, lonu, adj, xcol,
    pair_out, seg, segco, chipco, coin,
    s_out, s_in, x_out, x_in, unm, xlon,
    latc, latcx, lz_out, lz_in, lzx_out, lzx_in, sc_in, t_out, t_in, tx_out, tx_in,
    lsem, ssem, rsem,
):
    lon, lat = lax.axis_index("lon"), lax.axis_index("lat")
    core, chip = lax.rem(lon, 2), lon // 2
    other = 1 - core
    partner = {"lon": 2 * chip + other}
    chip_at = lambda k: lax.rem(chip + k, CHIPS)
    peer = lambda k: {"lon": 2 * chip_at(k) + core}
    lon_peer = lambda k: {"lon": lax.rem(lon + k, LONS)}
    lat_peer = lambda k: {"lat": lax.rem(lat + k, LATS)}

    barrier = pltpu.get_barrier_semaphore()
    greeted = [lon_peer(k) for k in FAR_LONS] + [lat_peer(k) for k in FAR_LATS]
    for device in greeted:
        pl.semaphore_signal(barrier, inc=1, device_id=device, device_id_type=MESH)

    loads = [pltpu.make_async_copy(a, b, lsem.at[i]) for i, (a, b) in enumerate(((lond, lond_v), (vert, vert_v), (latd, latd_v)))]
    for copy in loads:
        copy.start()
    parts = 4
    size = ROWS // parts
    big = []
    for i in range(parts):
        rows = pl.ds(i * size, size)
        big.append((
            pltpu.make_async_copy(inc.at[rows], inc_v.at[rows], lsem.at[3 + 2 * i]),
            pltpu.make_async_copy(std.at[rows], std_v.at[rows], lsem.at[4 + 2 * i]),
        ))
        for copy in big[-1]:
            copy.start()

    def send(src, dst, which, device):
        copy = pltpu.make_async_remote_copy(
            src_ref=src, dst_ref=dst, send_sem=ssem.at[which], recv_sem=rsem.at[which],
            device_id=device, device_id_type=MESH,
        )
        copy.start()

    def arrived(ref, which):
        pltpu.make_async_copy(ref, ref, rsem.at[which]).wait()

    def sent(ref, which):
        pltpu.make_async_copy(ref, ref, ssem.at[which]).wait()

    loads[0].wait()
    lanes = lambda h: pl.ds(h * LANES, LANES)
    lon_row = lambda i, h: lond_v[pl.ds(i, 1), lanes(h)]
    for h in HALF:
        ends = []
        line = [None] * NLON
        for k in STATES:
            y = one_hot(k)
            for i in range(NLON) if k % 2 == 0 else reversed(range(NLON)):
                d = lon_row(i, h)
                y = d * y if line[i] is None else d * y + (1.0 - d) * line[i]
                line[i] = y
            ends.append(y)
        for i in range(NLON):
            lonu[h, pl.ds(8 * i, 8), :] = line[i]
        e1, e2, e3, e4 = ends
        store_coefs(segco, (core, h), 0, (e1[0:1], e2[0:1], e3[1:2], e3[0:1], e4[1:2], e4[0:1]))

    loads[1].wait()
    zero64 = jnp.zeros((64, 64), F32)
    for p in range(2):
        a, b = vert_v[2 * p], vert_v[2 * p + 1]
        block = jnp.concatenate(
            [jnp.concatenate([a, zero64], axis=1), jnp.concatenate([zero64, b], axis=1)], axis=0
        )
        for factor, weight in ((block, vw), (block.T, tw)):
            high, low = split(factor)
            top = jnp.concatenate([high, low], axis=1)
            weight[p] = jnp.concatenate([top, jnp.concatenate([high, jnp.zeros_like(high)], axis=1)], axis=0)

    for i in range(parts):
        for copy in big[i]:
            copy.wait()
        rows = pl.ds(i * size, size)
        for h in HALF:
            work[h, rows, :] = dot3(inc_v[rows, lanes(h)] * std_v[rows, lanes(h)], vw[h])

    def lon_sweeps(half, put):
        first = half * (ROWS // 2)
        rows = lambda i: pl.ds(first + i, 32, stride=NLON)
        for k in STATES:
            ys = [jnp.zeros((32, LANES), F32)] * 2
            for i in range(NLON) if k % 2 == 0 else reversed(range(NLON)):
                for h in HALF:
                    u = work[h, rows(i), :] if k == 0 else temp[h, i]
                    d = lon_row(i, h)
                    ys[h] = d * ys[h] + (1.0 - d) * u
                    if k < 3:
                        temp[h, i] = ys[h]
                    else:
                        work[h, rows(i), :] = ys[h]
            for h in HALF:
                put(h, k, ys[h])

    def put_out(h, k, y):
        pair_out[h, k] = y

    def put_own(h, k, y):
        seg[core, h, k] = y

    lon_sweeps(other, put_out)
    pl.semaphore_wait(barrier, len(greeted))
    send(segco.at[core], segco.at[core], 0, partner)

    solves = lax.rem(lon, 8) // 2 == 1
    solvers = [(2 * k + h, h, 8 * k + 2 + h) for k in STATES for h in HALF]

    def to_solvers(out, into, which):
        for n, h, solver in solvers:
            place = lax.rem(lon - solver + LONS, LONS)

            @pl.when(place != 0)
            def _():
                send(out(n, h), into.at[place], which, {"lon": solver})

            @pl.when(place == 0)
            def _():
                into[0] = out(n, h)[...]

    to_solvers(lambda n, h: segco.at[core, h], sc_in, 8)
    send(pair_out, seg.at[core], 1, partner)

    loads[2].wait()
    adj[...] = jnp.zeros_like(adj)

    def adjoint(reverse, carry):
        def body(step, cs):
            cs = list(cs)
            first = pl.multiple_of((NLAT // 8 - 1 - step if reverse else step) * 8, 8)
            decays = [latd_v[pl.ds(first, 8), lanes(h)] for h in HALF]
            for j in reversed(range(8)) if reverse else range(8):
                at = pl.ds(pl.multiple_of((first + j) * 8, 8), 8)
                for h in HALF:
                    d = decays[h][j:j + 1]
                    t = adj[h, at, :] + cs[h]
                    adj[h, at, :] = (1.0 - d) * t
                    cs[h] = d * t
            return tuple(cs)

        return lax.fori_loop(0, NLAT // 8, body, tuple(carry))

    carried = [adjoint(k % 2 == 0, [one_hot(k)] * 2) for k in (3, 2, 1, 0)]
    for h in HALF:
        e1, e2 = carried[3][h], carried[2][h]
        store_coefs(latc, (lat, h), 16, (e1[0:1], e1[1:2], e2[2:3], e1[2:3], e2[3:4], e1[3:4]))

    arrived(segco.at[other], 0)
    co = lambda s, h, r: segco[s, h, pl.ds(r, 1), :]
    for h in HALF:
        g_l, a21_l, a32_l, a31_l, a42_l, a41_l = (co(0, h, r) for r in range(6))
        g_r, a21_r, a32_r, a31_r, a42_r, a41_r = (co(1, h, r) for r in range(6))
        b1 = a21_r * g_l
        f2 = a32_l * b1 + a31_l
        b2 = a21_r * f2 + a41_r * g_l
        f2b = a32_l * g_r
        values = (
            g_l * g_r,
            g_l * b1 + a21_l,
            g_r * f2b + a32_r,
            g_r * f2 + a31_r * g_l,
            g_l * (a21_r * f2b + a42_r) + a42_l * g_r,
            g_l * b2 + a42_l * b1 + a41_l,
        )
        for r, value in enumerate(values):
            chipco[h, pl.ds(r, 1), :] = value
        chipco[h, pl.ds(6, 2), :] = jnp.zeros((2, LANES), F32)
    coin[0] = chipco[chip // 8]
    for k in FAR_CHIPS:
        send(chipco.at[chip_at(k) // 8], coin.at[CHIPS - k], 2, peer(k))

    lon_sweeps(core, put_own)

    weights = [[[adj[h, pl.ds(256 * half + k, 32, stride=8), :] for k in STATES] for half in (core, other)] for h in HALF]
    for h in HALF:
        for c in STATES:
            own, rest = seg[core, h, c], pair_out[h, c]
            for k in STATES:
                total = weights[h][0][k] * own + weights[h][1][k] * rest
                latc[lat, h, pl.ds(4 * k + c, 1), :] = jnp.sum(total, axis=0, keepdims=True)
    for k in FAR_LATS:
        send(latc.at[lat], latc.at[lat], 7, lat_peer(k))

    arrived(seg.at[other], 1)
    def merge(h, left, right):
        g_l, a21_l, a32_l, a31_l, a42_l, a41_l = (co(0, h, r) for r in range(6))
        g_r, a21_r, a32_r, a31_r, a42_r, a41_r = (co(1, h, r) for r in range(6))
        (l1, l2, l3, l4), (r1, r2, r3, r4) = left, right
        b1 = a21_r * l1 + r2
        f2 = a32_l * b1 + l3
        b2 = a21_r * f2 + a41_r * l1 + r4
        return (
            g_r * l1 + r1,
            g_l * b1 + l2,
            g_r * f2 + a31_r * l1 + r3,
            g_l * b2 + a42_l * b1 + l4,
        )

    def unmerge(h, left, right, entering):
        g_l, a21_l, a32_l, a31_l, a42_l, a41_l = (co(0, h, r) for r in range(6))
        g_r, a21_r, a32_r, a31_r, a42_r, a41_r = (co(1, h, r) for r in range(6))
        (l1, l2, l3, l4), (r1, r2, r3, r4) = left, right
        e1, e2, e3, e4 = entering
        f1 = g_l * e1 + l1
        b1 = g_r * e2 + a21_r * f1 + r2
        f2 = g_l * e3 + a32_l * b1 + a31_l * e1 + l3
        b2 = g_r * e4 + a21_r * f2 + a42_r * e2 + a41_r * f1 + r4
        return (e1, b1, e3, b2), (f1, e2, f2, e4)

    states = lambda s, h: [seg[s, h, k] for k in STATES]
    for h in HALF:
        merged = merge(h, states(0, h), states(1, h))
        for k in STATES:
            for j in range(8):
                s_out[8 * h + j, k] = merged[k][4 * j:4 * j + 4]
    for k in FAR_CHIPS:
        send(s_out.at[chip_at(k)], s_in.at[CHIPS - k], 3, peer(k))
    s_in[0] = s_out[chip]

    latu[...] = jnp.zeros_like(latu)

    def lat_sweep(lines, reverse, carry):
        def body(step, ys):
            ys = list(ys)
            first = pl.multiple_of((NLAT // 8 - 1 - step if reverse else step) * 8, 8)
            decays = [latd_v[pl.ds(first, 8), lanes(h)] for h in HALF]
            for j in reversed(range(8)) if reverse else range(8):
                i = first + j
                for n, (ref, h, height) in enumerate(lines):
                    d = decays[h][j:j + 1]
                    at = pl.ds(pl.multiple_of(i * height, height), height)
                    ys[n] = d * ys[n] + (1.0 - d) * ref[h, at, :]
                    ref[h, at, :] = ys[n]
            return tuple(ys)

        return lax.fori_loop(0, NLAT // 8, body, tuple(carry))

    lines = [(work, 0, 16), (work, 1, 16), (latu, 0, 8), (latu, 1, 8)]
    ends = []
    for k in STATES:
        start = [jnp.zeros((16, LANES), F32)] * 2 + [one_hot(k)] * 2
        ends.append(lat_sweep(lines, k % 2 == 1, start))
    for n in range(LATS):
        for k in STATES:
            lz_out[n, k] = ends[k][n // 4][4 * (n % 4):4 * (n % 4) + 4]
    for k in FAR_LATS:
        send(lz_out.at[lax.rem(lat + k, LATS)], lz_in.at[lat], 4, lat_peer(k))
    lz_in[lat] = lz_out[lat]

    def lat_solve(state, coef, put, zero):
        x1, x2, x3, x4 = ([zero] * LATS for _ in STATES)
        for p in range(LATS - 1):
            x1[p + 1] = coef(p, 0) * x1[p] + state(p, 0)
        for p in range(LATS - 1, 0, -1):
            x2[p - 1] = coef(p, 0) * x2[p] + (coef(p, 1) * x1[p] + state(p, 1))
        for p in range(LATS - 1):
            x3[p + 1] = coef(p, 0) * x3[p] + (coef(p, 2) * x2[p] + coef(p, 3) * x1[p] + state(p, 2))
        for p in range(LATS - 1, 0, -1):
            x4[p - 1] = coef(p, 0) * x4[p] + (
                coef(p, 1) * x3[p] + coef(p, 4) * x2[p] + coef(p, 5) * x1[p] + state(p, 3)
            )
        for p in range(LATS):
            for k, x in enumerate((x1, x2, x3, x4)):
                put(p, k, x[p])

    arrived(latc.at[pl.ds(0, LATS - 1)], 7)
    for h in HALF:
        def put_c(p, k, x, h=h):
            latcx[p, h, pl.ds(4 * k, 4), :] = x

        lat_solve(
            lambda p, k: latc[p, h, pl.ds(4 * k, 4), :],
            lambda p, r: latc[p, h, pl.ds(16 + r, 1), :],
            put_c, jnp.zeros((4, LANES), F32),
        )
    for n, h, _ in solvers:
        t_out[n] = latcx[lat, h, pl.ds(4 * (n // 2), 4), :]
    to_solvers(lambda n, h: t_out.at[n], t_in, 9)

    seat = range(CHIPS)

    def ring_maps(seat, row):
        cc = [[row(j, r) for r in range(6)] for j in seat]
        ahead, behind = [jnp.ones((1, LANES), F32)], [jnp.ones((1, LANES), F32)]
        for j in seat:
            ahead.append(ahead[-1] * cc[j][0])
            behind.append(behind[-1] * cc[-1 - j][0])
        return cc, ahead, behind, 1.0 / (1.0 - ahead[-1])

    def ring_solve(seat, maps, state, zero):
        cc, ahead, behind, close = maps

        def ring(terms, reverse):
            t = zero
            before = [None] * len(seat)
            for j in reversed(seat) if reverse else seat:
                before[j] = t
                t = cc[j][0] * t + terms[j]
            start = t * close
            growth = (lambda j: behind[len(seat) - 1 - j]) if reverse else (lambda j: ahead[j])
            return [before[j] + growth(j) * start for j in seat]

        x1 = ring([state(j, 0) for j in seat], False)
        x2 = ring([state(j, 1) + cc[j][1] * x1[j] for j in seat], True)
        x3 = ring([state(j, 2) + cc[j][3] * x1[j] + cc[j][2] * x2[j] for j in seat], False)
        x4 = ring([state(j, 3) + cc[j][5] * x1[j] + cc[j][4] * x2[j] + cc[j][1] * x3[j] for j in seat], True)
        return x1, x2, x3, x4

    arrived(coin.at[pl.ds(1, CHIPS - 1)], 2)
    maps = ring_maps(seat, lambda j, r: coin[j, pl.ds(r, 1), :])
    arrived(s_in.at[pl.ds(1, CHIPS - 1)], 3)
    x1, x2, x3, x4 = ring_solve(seat, maps, lambda j, k: s_in[j, k], jnp.zeros((4, LANES), F32))
    for j in seat:
        for k, x in enumerate((x1, x2, x3, x4)):
            x_out[j, k] = x[j]
    for k in FAR_CHIPS:
        send(x_out.at[k], x_in.at[chip], 5, peer(k))
    x_in[chip] = x_out[0]

    @pl.when(solves)
    def _():
        devices = range(LONS)
        arrived(sc_in.at[pl.ds(1, LONS - 1)], 8)
        maps = ring_maps(devices, lambda j, r: sc_in[j, pl.ds(r, 1), :])
        arrived(t_in.at[pl.ds(1, LONS - 1)], 9)
        found = ring_solve(devices, maps, lambda j, c: t_in[j, pl.ds(c, 1), :], jnp.zeros((1, LANES), F32))
        for j in devices:
            for c in STATES:
                tx_out[j, pl.ds(c, 1), :] = found[c][j]
        for k in FAR_LONS:
            send(tx_out.at[k], tx_in.at[2 * (lon // 8) + core], 10, lon_peer(k))
        tx_in[2 * (lon // 8) + core] = tx_out[0]

    arrived(lz_in.at[pl.ds(0, LATS - 1)], 4)

    def put_z(p, k, x):
        lzx_out[p, k] = x

    lat_solve(
        lambda p, k: lz_in[p, k],
        lambda p, r: latc[p, lat // 4, pl.ds(16 + r, 1), :],
        put_z, jnp.zeros((4, LANES), F32),
    )
    for k in FAR_LATS:
        send(lzx_out.at[lax.rem(lat + k, LATS)], lzx_in.at[lat], 11, lat_peer(k))
    lzx_in[lat] = lzx_out[lat]

    arrived(x_in.at[pl.ds(0, CHIPS - 1)], 5)
    for h in HALF:
        entering = [jnp.concatenate([x_in[8 * h + j, k] for j in range(8)], axis=0) for k in STATES]
        for whose, parts_in in enumerate(unmerge(h, states(0, h), states(1, h), entering)):
            for k in STATES:
                unm[whose, h, k] = parts_in[k]
    send(unm.at[other], xlon.at[core], 6, partner)

    xlon[core] = unm[core]
    xcol[...] = jnp.zeros_like(xcol)
    arrived(xlon.at[other], 6)
    for h in HALF:
        for half in range(2):
            for c in STATES:
                xcol[h, pl.ds(256 * half + c, 32, stride=8), :] = xlon[half, h, c]
    lines = [(xcol, 0, 8), (xcol, 1, 8)]
    for k in STATES:
        lat_sweep(lines, k % 2 == 1, [jnp.zeros((8, LANES), F32)] * 2)
    lon_unit = [[lonu[h, pl.ds(c, NLON, stride=8), :] for c in STATES] for h in HALF]

    def add_lon(step, _):
        for j in range(4):
            i = step * 4 + j
            for h in HALF:
                at = pl.ds(pl.multiple_of(i * 16, 16), 16)
                y = work[h, at, :]
                column = xcol[h, pl.ds(pl.multiple_of(i * 8, 8), 8), :]
                for c in STATES:
                    y = y + column[c:c + 1] * lon_unit[h][c]
                work[h, at, :] = y
        return 0

    lax.fori_loop(0, NLAT // 4, add_lon, 0)

    arrived(lzx_in.at[pl.ds(0, LATS - 1)], 11)

    @pl.when(solves)
    def _():
        arrived(tx_in.at[pl.ds(0, 7)], 10)

    @pl.when(jnp.logical_not(solves))
    def _():
        arrived(tx_in, 10)

    for h in HALF:
        for k in STATES:
            x = jnp.concatenate([lzx_in[4 * h + g, k] for g in range(4)], axis=0)
            for c in STATES:
                x = x + lon_unit[h][c] * tx_in[2 * k + h, pl.ds(c, 1), :]
            enter[h, k] = x

    sent(segco.at[core], 0)
    sent(pair_out, 1)
    sent(coin.at[pl.ds(1, CHIPS - 1)], 2)
    sent(s_in.at[pl.ds(1, CHIPS - 1)], 3)
    sent(lz_in.at[pl.ds(0, LATS - 1)], 4)
    sent(x_in.at[pl.ds(0, CHIPS - 1)], 5)
    sent(unm.at[other], 6)
    sent(latc.at[pl.ds(0, LATS - 1)], 7)
    sent(lzx_in.at[pl.ds(0, LATS - 1)], 11)

    @pl.when(solves)
    def _():
        sent(sc_in.at[pl.ds(0, 7)], 8)
        sent(t_out.at[pl.ds(0, 7)], 9)
        sent(tx_out.at[pl.ds(1, LONS - 1)], 10)

    @pl.when(jnp.logical_not(solves))
    def _():
        sent(sc_in.at[pl.ds(0, 8)], 8)
        sent(t_out, 9)


def finish(work, latu, enter, std, tw, out, line, out_v, sem):
    parts = 4
    size = ROWS // parts

    for step in range(parts):
        rows = pl.ds(step * size, size)
        for h in HALF:
            for j in range(size // 16):
                i = step * (size // 16) + j
                y = work[h, pl.ds(i * 16, 16), :]
                unit = latu[h, pl.ds(i * 8, 8), :]
                for k in STATES:
                    y = y + unit[k:k + 1] * enter[h, k]
                line[h, pl.ds(16 * j, 16), :] = y
            lanes = pl.ds(h * LANES, LANES)
            out_v[rows, lanes] = std[rows, lanes] * dot3(line[h], tw[h])
        pltpu.make_async_copy(out_v.at[rows], out.at[rows], sem.at[0]).start()

    pltpu.make_async_copy(out_v, out, sem.at[0]).wait()


def per_device(increment, error_std, vertical, lon_decay, lat_decay):
    vmem = lambda *shape: pltpu.VMEM(shape, F32)
    whole = pl.BlockSpec(memory_space=pltpu.VMEM)
    weights = pltpu.VMEM((2, 256, 256), BF16)
    held = pl.pallas_call(
        kernel,
        out_shape=[
            vmem(2, ROWS, LANES), vmem(2, NLAT * 8, LANES), vmem(2, 4, NLON, LANES), vmem(ROWS, 256), weights,
        ],
        in_specs=[pl.BlockSpec(memory_space=pl.ANY)] * 5,
        out_specs=[whole] * 5,
        scratch_shapes=[
            vmem(ROWS, 256), vmem(4, 64, 64), vmem(NLON, 256), vmem(NLAT, 256),
            weights, vmem(2, NLON, 32, LANES), vmem(2, NLON * 8, LANES),
            *[vmem(2, NLAT * 8, LANES)] * 2,
            vmem(2, 4, 32, LANES), vmem(2, 2, 4, 32, LANES), vmem(2, 2, 8, LANES), vmem(2, 8, LANES), vmem(CHIPS, 8, LANES),
            *[vmem(CHIPS, 4, 4, LANES)] * 4,
            vmem(2, 2, 4, 32, LANES), vmem(2, 2, 4, 32, LANES),
            vmem(LATS, 2, 24, LANES), vmem(LATS, 2, 16, LANES), *[vmem(LATS, 4, 4, LANES)] * 4,
            vmem(LONS, 8, LANES), vmem(8, 4, LANES), vmem(LONS, 4, LANES), vmem(LONS, 4, LANES), vmem(8, 4, LANES),
            pltpu.SemaphoreType.DMA((11,)), pltpu.SemaphoreType.DMA((13,)), pltpu.SemaphoreType.DMA((13,)),
        ],
        compiler_params=pltpu.CompilerParams(
            collective_id=0, has_side_effects=True, vmem_limit_bytes=24 * 1024 * 1024
        ),
    )(*[
        pltpu.with_memory_space_constraint(x, pltpu.HBM)
        for x in (increment.reshape(ROWS, 256), error_std.reshape(ROWS, 256), vertical, lon_decay, lat_decay)
    ])
    result = pl.pallas_call(
        finish,
        out_shape=jax.ShapeDtypeStruct((ROWS, 256), F32),
        in_specs=[whole] * 5,
        out_specs=pl.BlockSpec(memory_space=pl.ANY),
        scratch_shapes=[vmem(2, ROWS // 4, LANES), vmem(ROWS, 256), pltpu.SemaphoreType.DMA((1,))],
        compiler_params=pltpu.CompilerParams(vmem_limit_bytes=24 * 1024 * 1024),
    )(*held)
    return result.reshape(NLAT, NLON, 256)


def solution(mesh):
    placed = (P("lat", "lon", None), P("lat", "lon", None), P(), P("lon", None), P("lat", None))
    return jax.shard_map(
        per_device, mesh=mesh, in_specs=placed, out_specs=P("lat", "lon", None), check_vma=False
    )
```

```python
import jax
import jax.numpy as jnp
from jax import lax
from jax.experimental import pallas as pl
from jax.experimental.pallas import tpu as pltpu
from jax.sharding import PartitionSpec as P

MESH = pl.DeviceIdType.MESH
F32 = jnp.float32
BF16 = jnp.bfloat16
NLAT, NLON, LANES = 64, 16, 128
ROWS = NLAT * NLON
LONS, CHIPS, LATS = 32, 16, 8
FAR_CHIPS = sorted(range(1, CHIPS), key=lambda k: -min(k, CHIPS - k))
FAR_LONS = sorted(range(1, LONS), key=lambda k: -min(k, LONS - k))
FAR_LATS = sorted(range(1, LATS), key=lambda k: -min(k, LATS - k))
HALF = range(2)
STATES = range(4)


def split(x):
    high = x.astype(BF16)
    return high, (x - high.astype(F32)).astype(BF16)


def dot3(x, weight):
    both = jnp.dot(jnp.concatenate(split(x), axis=1), weight, preferred_element_type=F32)
    return both[:, :LANES] + both[:, LANES:]


def one_hot(k):
    return jnp.where(lax.broadcasted_iota(jnp.int32, (8, LANES), 0) == k, 1.0, 0.0).astype(F32)


def store_coefs(ref, at, base, rows):
    for row, part in enumerate(rows):
        ref[(*at, pl.ds(base + row, 1), slice(None))] = part
    ref[(*at, pl.ds(base + 6, 2), slice(None))] = jnp.zeros((2, LANES), F32)


def kernel(
    inc, std, vert, lond, latd,
    work, latu, enter, std_v, tw,
    inc_v, vert_v, lond_v, latd_v,
    vw, temp, lonu, adj, xcol,
    pair_out, seg, segco,
    s_out, s_in, x_out, x_in, unm, xlon,
    latc, latcx, lz_out, lz_in, lzx_out, lzx_in, sc_in, t_out, t_in, tx_out, tx_in,
    lsem, ssem, rsem,
):
    lon, lat = lax.axis_index("lon"), lax.axis_index("lat")
    core, chip = lax.rem(lon, 2), lon // 2
    other = 1 - core
    partner = {"lon": 2 * chip + other}
    chip_at = lambda k: lax.rem(chip + k, CHIPS)
    peer = lambda k: {"lon": 2 * chip_at(k) + core}
    lon_peer = lambda k: {"lon": lax.rem(lon + k, LONS)}
    lat_peer = lambda k: {"lat": lax.rem(lat + k, LATS)}

    barrier = pltpu.get_barrier_semaphore()
    greeted = [lon_peer(k) for k in FAR_LONS] + [lat_peer(k) for k in FAR_LATS]
    for device in greeted:
        pl.semaphore_signal(barrier, inc=1, device_id=device, device_id_type=MESH)

    loads = [pltpu.make_async_copy(a, b, lsem.at[i]) for i, (a, b) in enumerate(((lond, lond_v), (vert, vert_v), (latd, latd_v)))]
    for copy in loads:
        copy.start()
    parts = 4
    size = ROWS // parts
    big = []
    for i in range(parts):
        rows = pl.ds(i * size, size)
        big.append((
            pltpu.make_async_copy(inc.at[rows], inc_v.at[rows], lsem.at[3 + 2 * i]),
            pltpu.make_async_copy(std.at[rows], std_v.at[rows], lsem.at[4 + 2 * i]),
        ))
        for copy in big[-1]:
            copy.start()

    def send(src, dst, which, device):
        copy = pltpu.make_async_remote_copy(
            src_ref=src, dst_ref=dst, send_sem=ssem.at[which], recv_sem=rsem.at[which],
            device_id=device, device_id_type=MESH,
        )
        copy.start()

    def arrived(ref, which):
        pltpu.make_async_copy(ref, ref, rsem.at[which]).wait()

    def sent(ref, which):
        pltpu.make_async_copy(ref, ref, ssem.at[which]).wait()

    loads[0].wait()
    lanes = lambda h: pl.ds(h * LANES, LANES)
    lon_row = lambda i, h: lond_v[pl.ds(i, 1), lanes(h)]
    for h in HALF:
        ends = []
        line = [None] * NLON
        for k in STATES:
            y = one_hot(k)
            for i in range(NLON) if k % 2 == 0 else reversed(range(NLON)):
                d = lon_row(i, h)
                y = d * y if line[i] is None else d * y + (1.0 - d) * line[i]
                line[i] = y
            ends.append(y)
        for i in range(NLON):
            lonu[h, pl.ds(8 * i, 8), :] = line[i]
        e1, e2, e3, e4 = ends
        store_coefs(segco, (core, h), 0, (e1[0:1], e2[0:1], e3[1:2], e3[0:1], e4[1:2], e4[0:1]))

    loads[1].wait()
    zero64 = jnp.zeros((64, 64), F32)
    for p in range(2):
        a, b = vert_v[2 * p], vert_v[2 * p + 1]
        block = jnp.concatenate(
            [jnp.concatenate([a, zero64], axis=1), jnp.concatenate([zero64, b], axis=1)], axis=0
        )
        for factor, weight in ((block, vw), (block.T, tw)):
            high, low = split(factor)
            top = jnp.concatenate([high, low], axis=1)
            weight[p] = jnp.concatenate([top, jnp.concatenate([high, jnp.zeros_like(high)], axis=1)], axis=0)

    for i in range(parts):
        for copy in big[i]:
            copy.wait()
        rows = pl.ds(i * size, size)
        for h in HALF:
            work[h, rows, :] = dot3(inc_v[rows, lanes(h)] * std_v[rows, lanes(h)], vw[h])

    def lon_sweeps(half, put):
        first = half * (ROWS // 2)
        rows = lambda i: pl.ds(first + i, 32, stride=NLON)
        for k in STATES:
            ys = [jnp.zeros((32, LANES), F32)] * 2
            for i in range(NLON) if k % 2 == 0 else reversed(range(NLON)):
                for h in HALF:
                    u = work[h, rows(i), :] if k == 0 else temp[h, i]
                    d = lon_row(i, h)
                    ys[h] = d * ys[h] + (1.0 - d) * u
                    if k < 3:
                        temp[h, i] = ys[h]
                    else:
                        work[h, rows(i), :] = ys[h]
            for h in HALF:
                put(h, k, ys[h])

    def put_out(h, k, y):
        pair_out[h, k] = y

    def put_own(h, k, y):
        seg[core, h, k] = y

    lon_sweeps(other, put_out)
    pl.semaphore_wait(barrier, len(greeted))
    send(segco.at[core], segco.at[core], 0, partner)
    send(pair_out, seg.at[core], 1, partner)

    lon_half = lambda l: lax.rem(l // 2, 2)
    for k in FAR_LONS:
        send(segco.at[core, lon_half(lax.rem(lon + k, LONS))], sc_in.at[LONS - k], 8, lon_peer(k))
    sc_in[0] = segco[core, lon_half(lon)]

    loads[2].wait()
    adj[...] = jnp.zeros_like(adj)

    def adjoint(reverse, carry):
        def body(step, cs):
            cs = list(cs)
            first = pl.multiple_of((NLAT // 8 - 1 - step if reverse else step) * 8, 8)
            decays = [latd_v[pl.ds(first, 8), lanes(h)] for h in HALF]
            for j in reversed(range(8)) if reverse else range(8):
                at = pl.ds(pl.multiple_of((first + j) * 8, 8), 8)
                for h in HALF:
                    d = decays[h][j:j + 1]
                    t = adj[h, at, :] + cs[h]
                    adj[h, at, :] = (1.0 - d) * t
                    cs[h] = d * t
            return tuple(cs)

        return lax.fori_loop(0, NLAT // 8, body, tuple(carry))

    carried = [adjoint(k % 2 == 0, [one_hot(k)] * 2) for k in (3, 2, 1, 0)]
    for h in HALF:
        e1, e2 = carried[3][h], carried[2][h]
        store_coefs(latc, (lat, h), 16, (e1[0:1], e1[1:2], e2[2:3], e1[2:3], e2[3:4], e1[3:4]))

    arrived(segco.at[other], 0)
    co = lambda s, h, r: segco[s, h, pl.ds(r, 1), :]

    def compose(left, right):
        g_l, a21_l, a32_l, a31_l, a42_l, a41_l = left
        g_r, a21_r, a32_r, a31_r, a42_r, a41_r = right
        b1 = a21_r * g_l
        f2 = a32_l * b1 + a31_l
        b2 = a21_r * f2 + a41_r * g_l
        f2b = a32_l * g_r
        return (
            g_l * g_r,
            g_l * b1 + a21_l,
            g_r * f2b + a32_r,
            g_r * f2 + a31_r * g_l,
            g_l * (a21_r * f2b + a42_r) + a42_l * g_r,
            g_l * b2 + a42_l * b1 + a41_l,
        )

    lon_sweeps(core, put_own)

    weights = [[[adj[h, pl.ds(256 * half + k, 32, stride=8), :] for k in STATES] for half in (core, other)] for h in HALF]
    for h in HALF:
        for c in STATES:
            own, rest = seg[core, h, c], pair_out[h, c]
            for k in STATES:
                total = weights[h][0][k] * own + weights[h][1][k] * rest
                latc[lat, h, pl.ds(4 * k + c, 1), :] = jnp.sum(total, axis=0, keepdims=True)
    for k in FAR_LATS:
        send(latc.at[lat], latc.at[lat], 7, lat_peer(k))

    arrived(seg.at[other], 1)
    def merge(h, left, right):
        g_l, a21_l, a32_l, a31_l, a42_l, a41_l = (co(0, h, r) for r in range(6))
        g_r, a21_r, a32_r, a31_r, a42_r, a41_r = (co(1, h, r) for r in range(6))
        (l1, l2, l3, l4), (r1, r2, r3, r4) = left, right
        b1 = a21_r * l1 + r2
        f2 = a32_l * b1 + l3
        b2 = a21_r * f2 + a41_r * l1 + r4
        return (
            g_r * l1 + r1,
            g_l * b1 + l2,
            g_r * f2 + a31_r * l1 + r3,
            g_l * b2 + a42_l * b1 + l4,
        )

    def unmerge(h, left, right, entering):
        g_l, a21_l, a32_l, a31_l, a42_l, a41_l = (co(0, h, r) for r in range(6))
        g_r, a21_r, a32_r, a31_r, a42_r, a41_r = (co(1, h, r) for r in range(6))
        (l1, l2, l3, l4), (r1, r2, r3, r4) = left, right
        e1, e2, e3, e4 = entering
        f1 = g_l * e1 + l1
        b1 = g_r * e2 + a21_r * f1 + r2
        f2 = g_l * e3 + a32_l * b1 + a31_l * e1 + l3
        b2 = g_r * e4 + a21_r * f2 + a42_r * e2 + a41_r * f1 + r4
        return (e1, b1, e3, b2), (f1, e2, f2, e4)

    states = lambda s, h: [seg[s, h, k] for k in STATES]
    for h in HALF:
        merged = merge(h, states(0, h), states(1, h))
        for k in STATES:
            for j in range(8):
                s_out[2 * j + h, k] = merged[k][4 * j:4 * j + 4]
    for k in FAR_CHIPS:
        send(s_out.at[chip_at(k)], s_in.at[CHIPS - k], 3, peer(k))
    s_in[0] = s_out[chip]

    latu[...] = jnp.zeros_like(latu)

    def lat_sweep(lines, reverse, carry):
        def body(step, ys):
            ys = list(ys)
            first = pl.multiple_of((NLAT // 8 - 1 - step if reverse else step) * 8, 8)
            decays = [latd_v[pl.ds(first, 8), lanes(h)] for h in HALF]
            for j in reversed(range(8)) if reverse else range(8):
                i = first + j
                for n, (ref, h, height) in enumerate(lines):
                    d = decays[h][j:j + 1]
                    at = pl.ds(pl.multiple_of(i * height, height), height)
                    ys[n] = d * ys[n] + (1.0 - d) * ref[h, at, :]
                    ref[h, at, :] = ys[n]
            return tuple(ys)

        return lax.fori_loop(0, NLAT // 8, body, tuple(carry))

    lines = [(work, 0, 16), (work, 1, 16), (latu, 0, 8), (latu, 1, 8)]
    ends = []
    for k in STATES:
        start = [jnp.zeros((16, LANES), F32)] * 2 + [one_hot(k)] * 2
        ends.append(lat_sweep(lines, k % 2 == 1, start))
    for n in range(LATS):
        for k in STATES:
            lz_out[n, k] = ends[k][n // 4][4 * (n % 4):4 * (n % 4) + 4]
    for k in FAR_LATS:
        send(lz_out.at[lax.rem(lat + k, LATS)], lz_in.at[lat], 4, lat_peer(k))
    lz_in[lat] = lz_out[lat]

    def lat_solve(state, coef, put, zero):
        x1, x2, x3, x4 = ([zero] * LATS for _ in STATES)
        for p in range(LATS - 1):
            x1[p + 1] = coef(p, 0) * x1[p] + state(p, 0)
        for p in range(LATS - 1, 0, -1):
            x2[p - 1] = coef(p, 0) * x2[p] + (coef(p, 1) * x1[p] + state(p, 1))
        for p in range(LATS - 1):
            x3[p + 1] = coef(p, 0) * x3[p] + (coef(p, 2) * x2[p] + coef(p, 3) * x1[p] + state(p, 2))
        for p in range(LATS - 1, 0, -1):
            x4[p - 1] = coef(p, 0) * x4[p] + (
                coef(p, 1) * x3[p] + coef(p, 4) * x2[p] + coef(p, 5) * x1[p] + state(p, 3)
            )
        for p in range(LATS):
            for k, x in enumerate((x1, x2, x3, x4)):
                put(p, k, x[p])

    arrived(latc.at[pl.ds(0, LATS - 1)], 7)
    for h in HALF:
        def put_c(p, k, x, h=h):
            latcx[p, h, pl.ds(4 * k, 4), :] = x

        lat_solve(
            lambda p, k: latc[p, h, pl.ds(4 * k, 4), :],
            lambda p, r: latc[p, h, pl.ds(16 + r, 1), :],
            put_c, jnp.zeros((4, LANES), F32),
        )
    place = lambda k, h: k % 2 + 2 * h + 4 * (k // 2)
    for k in STATES:
        for h in HALF:
            t_out[place(k, h)] = latcx[lat, h, pl.ds(4 * k, 4), :]
    for k in FAR_LONS:
        send(t_out.at[lax.rem(lon + k, 8)], t_in.at[LONS - k], 9, lon_peer(k))
    t_in[0] = t_out[lax.rem(lon, 8)]

    seat = range(CHIPS)

    def ring_maps(cc):
        seat = range(len(cc))
        ahead, behind = [jnp.ones((1, LANES), F32)], [jnp.ones((1, LANES), F32)]
        for j in seat:
            ahead.append(ahead[-1] * cc[j][0])
            behind.append(behind[-1] * cc[-1 - j][0])
        return cc, ahead, behind, 1.0 / (1.0 - ahead[-1])

    def ring_solve(seat, maps, state, zero):
        cc, ahead, behind, close = maps

        def ring(terms, reverse):
            t = zero
            before = [None] * len(seat)
            for j in reversed(seat) if reverse else seat:
                before[j] = t
                t = cc[j][0] * t + terms[j]
            start = t * close
            growth = (lambda j: behind[len(seat) - 1 - j]) if reverse else (lambda j: ahead[j])
            return [before[j] + growth(j) * start for j in seat]

        x1 = ring([state(j, 0) for j in seat], False)
        x2 = ring([state(j, 1) + cc[j][1] * x1[j] for j in seat], True)
        x3 = ring([state(j, 2) + cc[j][3] * x1[j] + cc[j][2] * x2[j] for j in seat], False)
        x4 = ring([state(j, 3) + cc[j][5] * x1[j] + cc[j][4] * x2[j] + cc[j][1] * x3[j] for j in seat], True)
        return x1, x2, x3, x4

    arrived(sc_in.at[pl.ds(1, LONS - 1)], 8)
    rows = lambda j: [sc_in[j, pl.ds(r, 1), :] for r in range(6)]
    left_at = lambda j: lax.rem(2 * j - core + LONS, LONS)
    maps = ring_maps([compose(rows(left_at(j)), rows(2 * j + 1 - core)) for j in seat])
    arrived(s_in.at[pl.ds(1, CHIPS - 1)], 3)
    x1, x2, x3, x4 = ring_solve(seat, maps, lambda j, k: s_in[j, k], jnp.zeros((4, LANES), F32))
    for j in seat:
        for k, x in enumerate((x1, x2, x3, x4)):
            x_out[j, k] = x[j]
    for k in FAR_CHIPS:
        send(x_out.at[k], x_in.at[chip], 5, peer(k))
    x_in[chip] = x_out[0]

    devices = range(LONS)
    maps = ring_maps([rows(j) for j in devices])
    arrived(t_in.at[pl.ds(1, LONS - 1)], 9)
    found = ring_solve(devices, maps, lambda j, c: t_in[j, pl.ds(c, 1), :], jnp.zeros((1, LANES), F32))
    for j in devices:
        for c in STATES:
            tx_out[j, pl.ds(c, 1), :] = found[c][j]
    for k in range(1, 8):
        near = 8 * (lon // 8) + lax.rem(lon + k, 8)
        send(tx_out.at[lax.rem(near - lon + LONS, LONS)], tx_in.at[lax.rem(lon, 8)], 10, {"lon": near})
    tx_in[lax.rem(lon, 8)] = tx_out[0]

    arrived(lz_in.at[pl.ds(0, LATS - 1)], 4)

    def put_z(p, k, x):
        lzx_out[p, k] = x

    lat_solve(
        lambda p, k: lz_in[p, k],
        lambda p, r: latc[p, lat // 4, pl.ds(16 + r, 1), :],
        put_z, jnp.zeros((4, LANES), F32),
    )
    for k in FAR_LATS:
        send(lzx_out.at[lax.rem(lat + k, LATS)], lzx_in.at[lat], 11, lat_peer(k))
    lzx_in[lat] = lzx_out[lat]

    arrived(x_in.at[pl.ds(0, CHIPS - 1)], 5)
    for h in HALF:
        entering = [jnp.concatenate([x_in[2 * j + h, k] for j in range(8)], axis=0) for k in STATES]
        for whose, parts_in in enumerate(unmerge(h, states(0, h), states(1, h), entering)):
            for k in STATES:
                unm[whose, h, k] = parts_in[k]
    send(unm.at[other], xlon.at[core], 6, partner)

    xlon[core] = unm[core]
    xcol[...] = jnp.zeros_like(xcol)
    arrived(xlon.at[other], 6)
    for h in HALF:
        for half in range(2):
            for c in STATES:
                xcol[h, pl.ds(256 * half + c, 32, stride=8), :] = xlon[half, h, c]
    lines = [(xcol, 0, 8), (xcol, 1, 8)]
    for k in STATES:
        lat_sweep(lines, k % 2 == 1, [jnp.zeros((8, LANES), F32)] * 2)
    lon_unit = [[lonu[h, pl.ds(c, NLON, stride=8), :] for c in STATES] for h in HALF]

    def add_lon(step, _):
        for j in range(4):
            i = step * 4 + j
            for h in HALF:
                at = pl.ds(pl.multiple_of(i * 16, 16), 16)
                y = work[h, at, :]
                column = xcol[h, pl.ds(pl.multiple_of(i * 8, 8), 8), :]
                for c in STATES:
                    y = y + column[c:c + 1] * lon_unit[h][c]
                work[h, at, :] = y
        return 0

    lax.fori_loop(0, NLAT // 4, add_lon, 0)

    arrived(lzx_in.at[pl.ds(0, LATS - 1)], 11)

    arrived(tx_in.at[pl.ds(0, 7)], 10)
    for h in HALF:
        for k in STATES:
            x = jnp.concatenate([lzx_in[4 * h + g, k] for g in range(4)], axis=0)
            for c in STATES:
                x = x + lon_unit[h][c] * tx_in[place(k, h), pl.ds(c, 1), :]
            enter[h, k] = x

    sent(segco.at[core], 0)
    sent(pair_out, 1)
    sent(s_in.at[pl.ds(1, CHIPS - 1)], 3)
    sent(lz_in.at[pl.ds(0, LATS - 1)], 4)
    sent(x_in.at[pl.ds(0, CHIPS - 1)], 5)
    sent(unm.at[other], 6)
    sent(latc.at[pl.ds(0, LATS - 1)], 7)
    sent(lzx_in.at[pl.ds(0, LATS - 1)], 11)

    sent(sc_in.at[pl.ds(1, LONS - 1)], 8)
    sent(t_in.at[pl.ds(1, LONS - 1)], 9)
    sent(tx_in.at[pl.ds(0, 7)], 10)


def finish(work, latu, enter, std, tw, out, line, out_v, sem):
    parts = 4
    size = ROWS // parts

    for step in range(parts):
        rows = pl.ds(step * size, size)
        for h in HALF:
            for j in range(size // 16):
                i = step * (size // 16) + j
                y = work[h, pl.ds(i * 16, 16), :]
                unit = latu[h, pl.ds(i * 8, 8), :]
                for k in STATES:
                    y = y + unit[k:k + 1] * enter[h, k]
                line[h, pl.ds(16 * j, 16), :] = y
            lanes = pl.ds(h * LANES, LANES)
            out_v[rows, lanes] = std[rows, lanes] * dot3(line[h], tw[h])
        pltpu.make_async_copy(out_v.at[rows], out.at[rows], sem.at[0]).start()

    pltpu.make_async_copy(out_v, out, sem.at[0]).wait()


def per_device(increment, error_std, vertical, lon_decay, lat_decay):
    vmem = lambda *shape: pltpu.VMEM(shape, F32)
    whole = pl.BlockSpec(memory_space=pltpu.VMEM)
    weights = pltpu.VMEM((2, 256, 256), BF16)
    held = pl.pallas_call(
        kernel,
        out_shape=[
            vmem(2, ROWS, LANES), vmem(2, NLAT * 8, LANES), vmem(2, 4, NLON, LANES), vmem(ROWS, 256), weights,
        ],
        in_specs=[pl.BlockSpec(memory_space=pl.ANY)] * 5,
        out_specs=[whole] * 5,
        scratch_shapes=[
            vmem(ROWS, 256), vmem(4, 64, 64), vmem(NLON, 256), vmem(NLAT, 256),
            weights, vmem(2, NLON, 32, LANES), vmem(2, NLON * 8, LANES),
            *[vmem(2, NLAT * 8, LANES)] * 2,
            vmem(2, 4, 32, LANES), vmem(2, 2, 4, 32, LANES), vmem(2, 2, 8, LANES),
            *[vmem(CHIPS, 4, 4, LANES)] * 4,
            vmem(2, 2, 4, 32, LANES), vmem(2, 2, 4, 32, LANES),
            vmem(LATS, 2, 24, LANES), vmem(LATS, 2, 16, LANES), *[vmem(LATS, 4, 4, LANES)] * 4,
            vmem(LONS, 8, LANES), vmem(8, 4, LANES), vmem(LONS, 4, LANES), vmem(LONS, 4, LANES), vmem(8, 4, LANES),
            pltpu.SemaphoreType.DMA((11,)), pltpu.SemaphoreType.DMA((13,)), pltpu.SemaphoreType.DMA((13,)),
        ],
        compiler_params=pltpu.CompilerParams(
            collective_id=0, has_side_effects=True, vmem_limit_bytes=24 * 1024 * 1024
        ),
    )(*[
        pltpu.with_memory_space_constraint(x, pltpu.HBM)
        for x in (increment.reshape(ROWS, 256), error_std.reshape(ROWS, 256), vertical, lon_decay, lat_decay)
    ])
    result = pl.pallas_call(
        finish,
        out_shape=jax.ShapeDtypeStruct((ROWS, 256), F32),
        in_specs=[whole] * 5,
        out_specs=pl.BlockSpec(memory_space=pl.ANY),
        scratch_shapes=[vmem(2, ROWS // 4, LANES), vmem(ROWS, 256), pltpu.SemaphoreType.DMA((1,))],
        compiler_params=pltpu.CompilerParams(vmem_limit_bytes=24 * 1024 * 1024),
    )(*held)
    return result.reshape(NLAT, NLON, 256)


def solution(mesh):
    placed = (P("lat", "lon", None), P("lat", "lon", None), P(), P("lon", None), P("lat", None))
    return jax.shard_map(
        per_device, mesh=mesh, in_specs=placed, out_specs=P("lat", "lon", None), check_vma=False
    )
```

```python
import jax
import jax.numpy as jnp
from jax import lax
from jax.experimental import pallas as pl
from jax.experimental.pallas import tpu as pltpu
from jax.sharding import PartitionSpec as P

MESH = pl.DeviceIdType.MESH
F32 = jnp.float32
BF16 = jnp.bfloat16
NLAT, NLON, LANES = 64, 16, 128
ROWS = NLAT * NLON
LONS, CHIPS, LATS = 32, 16, 8
FAR_CHIPS = sorted(range(1, CHIPS), key=lambda k: -min(k, CHIPS - k))
FAR_LONS = sorted(range(1, LONS), key=lambda k: -min(k, LONS - k))
FAR_LATS = sorted(range(1, LATS), key=lambda k: -min(k, LATS - k))
HALF = range(2)
STATES = range(4)


def split(x):
    high = x.astype(BF16)
    return high, (x - high.astype(F32)).astype(BF16)


def dot3(x, weight):
    both = jnp.dot(jnp.concatenate(split(x), axis=1), weight, preferred_element_type=F32)
    return both[:, :LANES] + both[:, LANES:]


def one_hot(k):
    return jnp.where(lax.broadcasted_iota(jnp.int32, (8, LANES), 0) == k, 1.0, 0.0).astype(F32)


def store_coefs(ref, at, base, rows):
    for row, part in enumerate(rows):
        ref[(*at, pl.ds(base + row, 1), slice(None))] = part
    ref[(*at, pl.ds(base + 6, 2), slice(None))] = jnp.zeros((2, LANES), F32)


def kernel(
    inc, std, vert, lond, latd,
    work, latu, enter, std_v, tw,
    inc_v, vert_v, lond_v, latd_v,
    vw, temp, lonu, adj, xcol,
    pair_out, seg, segco,
    s_out, s_in, x_out, x_in, unm, xlon,
    latc, latco, latcx, lz_out, lz_in, lzx_out, lzx_in, sc_in, t_out, t_in, tx_out, tx_in,
    lsem, ssem, rsem,
):
    lon, lat = lax.axis_index("lon"), lax.axis_index("lat")
    core, chip = lax.rem(lon, 2), lon // 2
    other = 1 - core
    partner = {"lon": 2 * chip + other}
    chip_at = lambda k: lax.rem(chip + k, CHIPS)
    peer = lambda k: {"lon": 2 * chip_at(k) + core}
    lon_peer = lambda k: {"lon": lax.rem(lon + k, LONS)}
    lat_peer = lambda k: {"lat": lax.rem(lat + k, LATS)}

    barrier = pltpu.get_barrier_semaphore()
    greeted = [lon_peer(k) for k in FAR_LONS] + [lat_peer(k) for k in FAR_LATS]
    for device in greeted:
        pl.semaphore_signal(barrier, inc=1, device_id=device, device_id_type=MESH)

    loads = [pltpu.make_async_copy(a, b, lsem.at[i]) for i, (a, b) in enumerate(((lond, lond_v), (vert, vert_v), (latd, latd_v)))]
    for copy in loads:
        copy.start()
    parts = 4
    size = ROWS // parts
    big = []
    for i in range(parts):
        rows = pl.ds(i * size, size)
        big.append((
            pltpu.make_async_copy(inc.at[rows], inc_v.at[rows], lsem.at[3 + 2 * i]),
            pltpu.make_async_copy(std.at[rows], std_v.at[rows], lsem.at[4 + 2 * i]),
        ))
        for copy in big[-1]:
            copy.start()

    def send(src, dst, which, device):
        copy = pltpu.make_async_remote_copy(
            src_ref=src, dst_ref=dst, send_sem=ssem.at[which], recv_sem=rsem.at[which],
            device_id=device, device_id_type=MESH,
        )
        copy.start()

    def arrived(ref, which):
        pltpu.make_async_copy(ref, ref, rsem.at[which]).wait()

    def sent(ref, which):
        pltpu.make_async_copy(ref, ref, ssem.at[which]).wait()

    loads[0].wait()
    lanes = lambda h: pl.ds(h * LANES, LANES)
    lon_row = lambda i, h: lond_v[pl.ds(i, 1), lanes(h)]
    for h in HALF:
        ends = []
        line = [None] * NLON
        for k in STATES:
            y = one_hot(k)
            for i in range(NLON) if k % 2 == 0 else reversed(range(NLON)):
                d = lon_row(i, h)
                y = d * y if line[i] is None else d * y + (1.0 - d) * line[i]
                line[i] = y
            ends.append(y)
        for i in range(NLON):
            lonu[h, pl.ds(8 * i, 8), :] = line[i]
        e1, e2, e3, e4 = ends
        store_coefs(segco, (core, h), 0, (e1[0:1], e2[0:1], e3[1:2], e3[0:1], e4[1:2], e4[0:1]))

    loads[1].wait()
    zero64 = jnp.zeros((64, 64), F32)
    for p in range(2):
        a, b = vert_v[2 * p], vert_v[2 * p + 1]
        block = jnp.concatenate(
            [jnp.concatenate([a, zero64], axis=1), jnp.concatenate([zero64, b], axis=1)], axis=0
        )
        for factor, weight in ((block, vw), (block.T, tw)):
            high, low = split(factor)
            top = jnp.concatenate([high, low], axis=1)
            weight[p] = jnp.concatenate([top, jnp.concatenate([high, jnp.zeros_like(high)], axis=1)], axis=0)

    for i in range(parts):
        for copy in big[i]:
            copy.wait()
        rows = pl.ds(i * size, size)
        for h in HALF:
            work[h, rows, :] = dot3(inc_v[rows, lanes(h)] * std_v[rows, lanes(h)], vw[h])

    def lon_sweeps(half, put):
        first = half * (ROWS // 2)
        rows = lambda i: pl.ds(first + i, 32, stride=NLON)
        for k in STATES:
            ys = [jnp.zeros((32, LANES), F32)] * 2
            for i in range(NLON) if k % 2 == 0 else reversed(range(NLON)):
                for h in HALF:
                    u = work[h, rows(i), :] if k == 0 else temp[h, i]
                    d = lon_row(i, h)
                    ys[h] = d * ys[h] + (1.0 - d) * u
                    if k < 3:
                        temp[h, i] = ys[h]
                    else:
                        work[h, rows(i), :] = ys[h]
            for h in HALF:
                put(h, k, ys[h])

    def put_out(h, k, y):
        pair_out[h, k] = y

    def put_own(h, k, y):
        seg[core, h, k] = y

    lon_sweeps(other, put_out)
    pl.semaphore_wait(barrier, len(greeted))
    send(segco.at[core], segco.at[core], 0, partner)
    send(pair_out, seg.at[core], 1, partner)

    for k in FAR_CHIPS:
        send(segco.at[core, lax.rem(chip + k, 2)], sc_in.at[core, CHIPS - k], 8, peer(k))
    sc_in[core, 0] = segco[core, lax.rem(chip, 2)]

    loads[2].wait()
    adj[...] = jnp.zeros_like(adj)

    def adjoint(reverse, carry):
        def body(step, cs):
            cs = list(cs)
            first = pl.multiple_of((NLAT // 8 - 1 - step if reverse else step) * 8, 8)
            decays = [latd_v[pl.ds(first, 8), lanes(h)] for h in HALF]
            for j in reversed(range(8)) if reverse else range(8):
                at = pl.ds(pl.multiple_of((first + j) * 8, 8), 8)
                for h in HALF:
                    d = decays[h][j:j + 1]
                    t = adj[h, at, :] + cs[h]
                    adj[h, at, :] = (1.0 - d) * t
                    cs[h] = d * t
            return tuple(cs)

        return lax.fori_loop(0, NLAT // 8, body, tuple(carry))

    carried = [adjoint(k % 2 == 0, [one_hot(k)] * 2) for k in (3, 2, 1, 0)]
    for h in HALF:
        e1, e2 = carried[3][h], carried[2][h]
        store_coefs(latco, (lat, h), 0, (e1[0:1], e1[1:2], e2[2:3], e1[2:3], e2[3:4], e1[3:4]))
    for k in FAR_LATS:
        send(latco.at[lat], latco.at[lat], 12, lat_peer(k))

    arrived(segco.at[other], 0)
    co = lambda s, h, r: segco[s, h, pl.ds(r, 1), :]

    def compose(left, right):
        g_l, a21_l, a32_l, a31_l, a42_l, a41_l = left
        g_r, a21_r, a32_r, a31_r, a42_r, a41_r = right
        b1 = a21_r * g_l
        f2 = a32_l * b1 + a31_l
        b2 = a21_r * f2 + a41_r * g_l
        f2b = a32_l * g_r
        return (
            g_l * g_r,
            g_l * b1 + a21_l,
            g_r * f2b + a32_r,
            g_r * f2 + a31_r * g_l,
            g_l * (a21_r * f2b + a42_r) + a42_l * g_r,
            g_l * b2 + a42_l * b1 + a41_l,
        )

    lon_sweeps(core, put_own)

    weights = [[[adj[h, pl.ds(256 * half + k, 32, stride=8), :] for k in STATES] for half in (core, other)] for h in HALF]
    for h in HALF:
        for c in STATES:
            own, rest = seg[core, h, c], pair_out[h, c]
            for k in STATES:
                total = weights[h][0][k] * own + weights[h][1][k] * rest
                latc[lat, h, pl.ds(4 * k + c, 1), :] = jnp.sum(total, axis=0, keepdims=True)
    for k in FAR_LATS:
        send(latc.at[lat], latc.at[lat], 7, lat_peer(k))

    arrived(seg.at[other], 1)
    def merge(h, left, right):
        g_l, a21_l, a32_l, a31_l, a42_l, a41_l = (co(0, h, r) for r in range(6))
        g_r, a21_r, a32_r, a31_r, a42_r, a41_r = (co(1, h, r) for r in range(6))
        (l1, l2, l3, l4), (r1, r2, r3, r4) = left, right
        b1 = a21_r * l1 + r2
        f2 = a32_l * b1 + l3
        b2 = a21_r * f2 + a41_r * l1 + r4
        return (
            g_r * l1 + r1,
            g_l * b1 + l2,
            g_r * f2 + a31_r * l1 + r3,
            g_l * b2 + a42_l * b1 + l4,
        )

    def unmerge(h, left, right, entering):
        g_l, a21_l, a32_l, a31_l, a42_l, a41_l = (co(0, h, r) for r in range(6))
        g_r, a21_r, a32_r, a31_r, a42_r, a41_r = (co(1, h, r) for r in range(6))
        (l1, l2, l3, l4), (r1, r2, r3, r4) = left, right
        e1, e2, e3, e4 = entering
        f1 = g_l * e1 + l1
        b1 = g_r * e2 + a21_r * f1 + r2
        f2 = g_l * e3 + a32_l * b1 + a31_l * e1 + l3
        b2 = g_r * e4 + a21_r * f2 + a42_r * e2 + a41_r * f1 + r4
        return (e1, b1, e3, b2), (f1, e2, f2, e4)

    states = lambda s, h: [seg[s, h, k] for k in STATES]
    for h in HALF:
        merged = merge(h, states(0, h), states(1, h))
        for k in STATES:
            for j in range(8):
                s_out[2 * j + h, k] = merged[k][4 * j:4 * j + 4]
    for k in FAR_CHIPS:
        send(s_out.at[chip_at(k)], s_in.at[CHIPS - k], 3, peer(k))
    s_in[0] = s_out[chip]

    latu[...] = jnp.zeros_like(latu)

    def lat_sweep(lines, reverse, carry):
        def body(step, ys):
            ys = list(ys)
            first = pl.multiple_of((NLAT // 8 - 1 - step if reverse else step) * 8, 8)
            decays = [latd_v[pl.ds(first, 8), lanes(h)] for h in HALF]
            for j in reversed(range(8)) if reverse else range(8):
                i = first + j
                for n, (ref, h, height) in enumerate(lines):
                    d = decays[h][j:j + 1]
                    at = pl.ds(pl.multiple_of(i * height, height), height)
                    ys[n] = d * ys[n] + (1.0 - d) * ref[h, at, :]
                    ref[h, at, :] = ys[n]
            return tuple(ys)

        return lax.fori_loop(0, NLAT // 8, body, tuple(carry))

    lines = [(work, 0, 16), (work, 1, 16), (latu, 0, 8), (latu, 1, 8)]
    ends = []
    for k in STATES:
        start = [jnp.zeros((16, LANES), F32)] * 2 + [one_hot(k)] * 2
        ends.append(lat_sweep(lines, k % 2 == 1, start))
    for n in range(LATS):
        for k in STATES:
            lz_out[n, k] = ends[k][n // 4][4 * (n % 4):4 * (n % 4) + 4]
    for k in FAR_LATS:
        send(lz_out.at[lax.rem(lat + k, LATS)], lz_in.at[lat], 4, lat_peer(k))
    lz_in[lat] = lz_out[lat]

    arrived(sc_in.at[core, pl.ds(1, CHIPS - 1)], 8)
    send(sc_in.at[core], sc_in.at[core], 2, partner)

    def lat_solve(state, coef, put, zero):
        x1, x2, x3, x4 = ([zero] * LATS for _ in STATES)
        for p in range(LATS - 1):
            x1[p + 1] = coef(p, 0) * x1[p] + state(p, 0)
        for p in range(LATS - 1, 0, -1):
            x2[p - 1] = coef(p, 0) * x2[p] + (coef(p, 1) * x1[p] + state(p, 1))
        for p in range(LATS - 1):
            x3[p + 1] = coef(p, 0) * x3[p] + (coef(p, 2) * x2[p] + coef(p, 3) * x1[p] + state(p, 2))
        for p in range(LATS - 1, 0, -1):
            x4[p - 1] = coef(p, 0) * x4[p] + (
                coef(p, 1) * x3[p] + coef(p, 4) * x2[p] + coef(p, 5) * x1[p] + state(p, 3)
            )
        for p in range(LATS):
            for k, x in enumerate((x1, x2, x3, x4)):
                put(p, k, x[p])

    arrived(latco.at[pl.ds(0, LATS - 1)], 12)
    arrived(latc.at[pl.ds(0, LATS - 1)], 7)
    for h in HALF:
        def put_c(p, k, x, h=h):
            latcx[p, h, pl.ds(4 * k, 4), :] = x

        lat_solve(
            lambda p, k: latc[p, h, pl.ds(4 * k, 4), :],
            lambda p, r: latco[p, h, pl.ds(r, 1), :],
            put_c, jnp.zeros((4, LANES), F32),
        )
    place = lambda k, h: k % 2 + 2 * h + 4 * (k // 2)
    for k in STATES:
        for h in HALF:
            t_out[place(k, h)] = latcx[lat, h, pl.ds(4 * k, 4), :]
    for k in FAR_LONS:
        send(t_out.at[lax.rem(lon + k, 8)], t_in.at[LONS - k], 9, lon_peer(k))
    t_in[0] = t_out[lax.rem(lon, 8)]

    seat = range(CHIPS)

    def ring_maps(cc):
        seat = range(len(cc))
        ahead, behind = [jnp.ones((1, LANES), F32)], [jnp.ones((1, LANES), F32)]
        for j in seat:
            ahead.append(ahead[-1] * cc[j][0])
            behind.append(behind[-1] * cc[-1 - j][0])
        return cc, ahead, behind, 1.0 / (1.0 - ahead[-1])

    def ring_solve(seat, maps, state, zero):
        cc, ahead, behind, close = maps

        def ring(terms, reverse):
            t = zero
            before = [None] * len(seat)
            for j in reversed(seat) if reverse else seat:
                before[j] = t
                t = cc[j][0] * t + terms[j]
            start = t * close
            growth = (lambda j: behind[len(seat) - 1 - j]) if reverse else (lambda j: ahead[j])
            return [before[j] + growth(j) * start for j in seat]

        x1 = ring([state(j, 0) for j in seat], False)
        x2 = ring([state(j, 1) + cc[j][1] * x1[j] for j in seat], True)
        x3 = ring([state(j, 2) + cc[j][3] * x1[j] + cc[j][2] * x2[j] for j in seat], False)
        x4 = ring([state(j, 3) + cc[j][5] * x1[j] + cc[j][4] * x2[j] + cc[j][1] * x3[j] for j in seat], True)
        return x1, x2, x3, x4

    arrived(sc_in.at[other], 2)
    rows = lambda c, j: [sc_in[c, j, pl.ds(r, 1), :] for r in range(6)]
    maps = ring_maps([compose(rows(0, j), rows(1, j)) for j in seat])
    arrived(s_in.at[pl.ds(1, CHIPS - 1)], 3)
    x1, x2, x3, x4 = ring_solve(seat, maps, lambda j, k: s_in[j, k], jnp.zeros((4, LANES), F32))
    for j in seat:
        for k, x in enumerate((x1, x2, x3, x4)):
            x_out[j, k] = x[j]
    for k in FAR_CHIPS:
        send(x_out.at[k], x_in.at[chip], 5, peer(k))
    x_in[chip] = x_out[0]

    devices = range(LONS)
    maps = ring_maps([rows(lax.rem(core + j, 2), lax.rem((core + j) // 2, CHIPS)) for j in devices])
    arrived(t_in.at[pl.ds(1, LONS - 1)], 9)
    found = ring_solve(devices, maps, lambda j, c: t_in[j, pl.ds(c, 1), :], jnp.zeros((1, LANES), F32))
    for j in devices:
        for c in STATES:
            tx_out[j, pl.ds(c, 1), :] = found[c][j]
    for k in range(1, 8):
        near = 8 * (lon // 8) + lax.rem(lon + k, 8)
        send(tx_out.at[lax.rem(near - lon + LONS, LONS)], tx_in.at[lax.rem(lon, 8)], 10, {"lon": near})
    tx_in[lax.rem(lon, 8)] = tx_out[0]

    arrived(lz_in.at[pl.ds(0, LATS - 1)], 4)

    def put_z(p, k, x):
        lzx_out[p, k] = x

    lat_solve(
        lambda p, k: lz_in[p, k],
        lambda p, r: latco[p, lat // 4, pl.ds(r, 1), :],
        put_z, jnp.zeros((4, LANES), F32),
    )
    for k in FAR_LATS:
        send(lzx_out.at[lax.rem(lat + k, LATS)], lzx_in.at[lat], 11, lat_peer(k))
    lzx_in[lat] = lzx_out[lat]

    arrived(x_in.at[pl.ds(0, CHIPS - 1)], 5)
    for h in HALF:
        entering = [jnp.concatenate([x_in[2 * j + h, k] for j in range(8)], axis=0) for k in STATES]
        for whose, parts_in in enumerate(unmerge(h, states(0, h), states(1, h), entering)):
            for k in STATES:
                unm[whose, h, k] = parts_in[k]
    send(unm.at[other], xlon.at[core], 6, partner)

    xlon[core] = unm[core]
    xcol[...] = jnp.zeros_like(xcol)
    arrived(xlon.at[other], 6)
    for h in HALF:
        for half in range(2):
            for c in STATES:
                xcol[h, pl.ds(256 * half + c, 32, stride=8), :] = xlon[half, h, c]
    lines = [(xcol, 0, 8), (xcol, 1, 8)]
    for k in STATES:
        lat_sweep(lines, k % 2 == 1, [jnp.zeros((8, LANES), F32)] * 2)
    lon_unit = [[lonu[h, pl.ds(c, NLON, stride=8), :] for c in STATES] for h in HALF]

    def add_lon(step, _):
        for j in range(4):
            i = step * 4 + j
            for h in HALF:
                at = pl.ds(pl.multiple_of(i * 16, 16), 16)
                y = work[h, at, :]
                column = xcol[h, pl.ds(pl.multiple_of(i * 8, 8), 8), :]
                for c in STATES:
                    y = y + column[c:c + 1] * lon_unit[h][c]
                work[h, at, :] = y
        return 0

    lax.fori_loop(0, NLAT // 4, add_lon, 0)

    arrived(lzx_in.at[pl.ds(0, LATS - 1)], 11)

    arrived(tx_in.at[pl.ds(0, 7)], 10)
    for h in HALF:
        for k in STATES:
            x = jnp.concatenate([lzx_in[4 * h + g, k] for g in range(4)], axis=0)
            for c in STATES:
                x = x + lon_unit[h][c] * tx_in[place(k, h), pl.ds(c, 1), :]
            enter[h, k] = x

    sent(segco.at[core], 0)
    sent(pair_out, 1)
    sent(s_in.at[pl.ds(1, CHIPS - 1)], 3)
    sent(lz_in.at[pl.ds(0, LATS - 1)], 4)
    sent(x_in.at[pl.ds(0, CHIPS - 1)], 5)
    sent(unm.at[other], 6)
    sent(latc.at[pl.ds(0, LATS - 1)], 7)
    sent(latco.at[pl.ds(0, LATS - 1)], 12)
    sent(lzx_in.at[pl.ds(0, LATS - 1)], 11)

    sent(sc_in.at[core], 2)
    sent(sc_in.at[core, pl.ds(1, CHIPS - 1)], 8)
    sent(t_in.at[pl.ds(1, LONS - 1)], 9)
    sent(tx_in.at[pl.ds(0, 7)], 10)


def finish(work, latu, enter, std, tw, out, line, out_v, sem):
    parts = 4
    size = ROWS // parts

    for step in range(parts):
        rows = pl.ds(step * size, size)
        for h in HALF:
            for j in range(size // 16):
                i = step * (size // 16) + j
                y = work[h, pl.ds(i * 16, 16), :]
                unit = latu[h, pl.ds(i * 8, 8), :]
                for k in STATES:
                    y = y + unit[k:k + 1] * enter[h, k]
                line[h, pl.ds(16 * j, 16), :] = y
            lanes = pl.ds(h * LANES, LANES)
            out_v[rows, lanes] = std[rows, lanes] * dot3(line[h], tw[h])
        pltpu.make_async_copy(out_v.at[rows], out.at[rows], sem.at[0]).start()

    pltpu.make_async_copy(out_v, out, sem.at[0]).wait()


def per_device(increment, error_std, vertical, lon_decay, lat_decay):
    vmem = lambda *shape: pltpu.VMEM(shape, F32)
    whole = pl.BlockSpec(memory_space=pltpu.VMEM)
    weights = pltpu.VMEM((2, 256, 256), BF16)
    held = pl.pallas_call(
        kernel,
        out_shape=[
            vmem(2, ROWS, LANES), vmem(2, NLAT * 8, LANES), vmem(2, 4, NLON, LANES), vmem(ROWS, 256), weights,
        ],
        in_specs=[pl.BlockSpec(memory_space=pl.ANY)] * 5,
        out_specs=[whole] * 5,
        scratch_shapes=[
            vmem(ROWS, 256), vmem(4, 64, 64), vmem(NLON, 256), vmem(NLAT, 256),
            weights, vmem(2, NLON, 32, LANES), vmem(2, NLON * 8, LANES),
            *[vmem(2, NLAT * 8, LANES)] * 2,
            vmem(2, 4, 32, LANES), vmem(2, 2, 4, 32, LANES), vmem(2, 2, 8, LANES),
            *[vmem(CHIPS, 4, 4, LANES)] * 4,
            vmem(2, 2, 4, 32, LANES), vmem(2, 2, 4, 32, LANES),
            vmem(LATS, 2, 16, LANES), vmem(LATS, 2, 8, LANES), vmem(LATS, 2, 16, LANES), *[vmem(LATS, 4, 4, LANES)] * 4,
            vmem(2, CHIPS, 8, LANES), vmem(8, 4, LANES), vmem(LONS, 4, LANES), vmem(LONS, 4, LANES), vmem(8, 4, LANES),
            pltpu.SemaphoreType.DMA((11,)), pltpu.SemaphoreType.DMA((13,)), pltpu.SemaphoreType.DMA((13,)),
        ],
        compiler_params=pltpu.CompilerParams(
            collective_id=0, has_side_effects=True, vmem_limit_bytes=24 * 1024 * 1024
        ),
    )(*[
        pltpu.with_memory_space_constraint(x, pltpu.HBM)
        for x in (increment.reshape(ROWS, 256), error_std.reshape(ROWS, 256), vertical, lon_decay, lat_decay)
    ])
    result = pl.pallas_call(
        finish,
        out_shape=jax.ShapeDtypeStruct((ROWS, 256), F32),
        in_specs=[whole] * 5,
        out_specs=pl.BlockSpec(memory_space=pl.ANY),
        scratch_shapes=[vmem(2, ROWS // 4, LANES), vmem(ROWS, 256), pltpu.SemaphoreType.DMA((1,))],
        compiler_params=pltpu.CompilerParams(vmem_limit_bytes=24 * 1024 * 1024),
    )(*held)
    return result.reshape(NLAT, NLON, 256)


def solution(mesh):
    placed = (P("lat", "lon", None), P("lat", "lon", None), P(), P("lon", None), P("lat", None))
    return jax.shard_map(
        per_device, mesh=mesh, in_specs=placed, out_specs=P("lat", "lon", None), check_vma=False
    )
```

```python
import jax
import jax.numpy as jnp
from jax import lax
from jax.experimental import pallas as pl
from jax.experimental.pallas import tpu as pltpu
from jax.sharding import PartitionSpec as P

MESH = pl.DeviceIdType.MESH
F32 = jnp.float32
BF16 = jnp.bfloat16
NLAT, NLON, LANES = 64, 16, 128
ROWS = NLAT * NLON
LONS, CHIPS, LATS = 32, 16, 8
FAR_CHIPS = sorted(range(1, CHIPS), key=lambda k: -min(k, CHIPS - k))
FAR_LONS = sorted(range(1, LONS), key=lambda k: -min(k, LONS - k))
FAR_LATS = sorted(range(1, LATS), key=lambda k: -min(k, LATS - k))
HALF = range(2)
STATES = range(4)


def split(x):
    high = x.astype(BF16)
    return high, (x - high.astype(F32)).astype(BF16)


def dot3(x, weight):
    both = jnp.dot(jnp.concatenate(split(x), axis=1), weight, preferred_element_type=F32)
    return both[:, :LANES] + both[:, LANES:]


def one_hot(k):
    return jnp.where(lax.broadcasted_iota(jnp.int32, (8, LANES), 0) == k, 1.0, 0.0).astype(F32)


def store_coefs(ref, at, base, rows):
    for row, part in enumerate(rows):
        ref[(*at, pl.ds(base + row, 1), slice(None))] = part
    ref[(*at, pl.ds(base + 6, 2), slice(None))] = jnp.zeros((2, LANES), F32)


def kernel(
    inc, std, vert, lond, latd,
    work, latu, enter, std_v, tw,
    inc_v, vert_v, lond_v, latd_v,
    vw, temp, lonu, adj, xcol,
    pair_out, seg, segco,
    s_out, s_in, x_out, x_in, unm, xlon,
    latc, latco, latcx, lz_out, lz_in, lzx_out, lzx_in, sc_in, t_out, t_in, tx_out, tx_in,
    lsem, ssem, rsem,
):
    lon, lat = lax.axis_index("lon"), lax.axis_index("lat")
    core, chip = lax.rem(lon, 2), lon // 2
    other = 1 - core
    partner = {"lon": 2 * chip + other}
    chip_at = lambda k: lax.rem(chip + k, CHIPS)
    peer = lambda k: {"lon": 2 * chip_at(k) + core}
    lon_peer = lambda k: {"lon": lax.rem(lon + k, LONS)}
    lat_peer = lambda k: {"lat": lax.rem(lat + k, LATS)}

    barrier = pltpu.get_barrier_semaphore()
    greeted = [lon_peer(k) for k in FAR_LONS] + [lat_peer(k) for k in FAR_LATS]
    for device in greeted:
        pl.semaphore_signal(barrier, inc=1, device_id=device, device_id_type=MESH)

    loads = [pltpu.make_async_copy(a, b, lsem.at[i]) for i, (a, b) in enumerate(((lond, lond_v), (vert, vert_v), (latd, latd_v)))]
    for copy in loads:
        copy.start()
    parts = 4
    size = ROWS // parts
    big = []
    for i in range(parts):
        rows = pl.ds(i * size, size)
        big.append((
            pltpu.make_async_copy(inc.at[rows], inc_v.at[rows], lsem.at[3 + 2 * i]),
            pltpu.make_async_copy(std.at[rows], std_v.at[rows], lsem.at[4 + 2 * i]),
        ))
        for copy in big[-1]:
            copy.start()

    def send(src, dst, which, device):
        copy = pltpu.make_async_remote_copy(
            src_ref=src, dst_ref=dst, send_sem=ssem.at[which], recv_sem=rsem.at[which],
            device_id=device, device_id_type=MESH,
        )
        copy.start()

    def arrived(ref, which):
        pltpu.make_async_copy(ref, ref, rsem.at[which]).wait()

    def sent(ref, which):
        pltpu.make_async_copy(ref, ref, ssem.at[which]).wait()

    loads[0].wait()
    lanes = lambda h: pl.ds(h * LANES, LANES)
    lon_row = lambda i, h: lond_v[pl.ds(i, 1), lanes(h)]
    for h in HALF:
        ends = []
        line = [None] * NLON
        for k in STATES:
            y = one_hot(k)
            for i in range(NLON) if k % 2 == 0 else reversed(range(NLON)):
                d = lon_row(i, h)
                y = d * y if line[i] is None else d * y + (1.0 - d) * line[i]
                line[i] = y
            ends.append(y)
        for i in range(NLON):
            lonu[h, pl.ds(8 * i, 8), :] = line[i]
        e1, e2, e3, e4 = ends
        store_coefs(segco, (core, h), 0, (e1[0:1], e2[0:1], e3[1:2], e3[0:1], e4[1:2], e4[0:1]))

    loads[1].wait()
    zero64 = jnp.zeros((64, 64), F32)
    for p in range(2):
        a, b = vert_v[2 * p], vert_v[2 * p + 1]
        block = jnp.concatenate(
            [jnp.concatenate([a, zero64], axis=1), jnp.concatenate([zero64, b], axis=1)], axis=0
        )
        for factor, weight in ((block, vw), (block.T, tw)):
            high, low = split(factor)
            top = jnp.concatenate([high, low], axis=1)
            weight[p] = jnp.concatenate([top, jnp.concatenate([high, jnp.zeros_like(high)], axis=1)], axis=0)

    for i in range(parts):
        for copy in big[i]:
            copy.wait()
        rows = pl.ds(i * size, size)
        for h in HALF:
            work[h, rows, :] = dot3(inc_v[rows, lanes(h)] * std_v[rows, lanes(h)], vw[h])

    def lon_sweeps(half, put):
        first = half * (ROWS // 2)
        rows = lambda i: pl.ds(first + i, 32, stride=NLON)
        for k in STATES:
            ys = [jnp.zeros((32, LANES), F32)] * 2
            for i in range(NLON) if k % 2 == 0 else reversed(range(NLON)):
                for h in HALF:
                    u = work[h, rows(i), :] if k == 0 else temp[h, i]
                    d = lon_row(i, h)
                    ys[h] = d * ys[h] + (1.0 - d) * u
                    if k < 3:
                        temp[h, i] = ys[h]
                    else:
                        work[h, rows(i), :] = ys[h]
            for h in HALF:
                put(h, k, ys[h])

    def put_out(h, k, y):
        pair_out[h, k] = y

    def put_own(h, k, y):
        seg[core, h, k] = y

    lon_sweeps(other, put_out)
    pl.semaphore_wait(barrier, len(greeted))
    send(pair_out, seg.at[core], 1, partner)
    send(segco.at[core], segco.at[core], 0, partner)

    for k in FAR_CHIPS:
        send(segco.at[core, lax.rem(chip + k, 2)], sc_in.at[core, CHIPS - k], 8, peer(k))
    sc_in[core, 0] = segco[core, lax.rem(chip, 2)]

    loads[2].wait()
    adj[...] = jnp.zeros_like(adj)

    def adjoint(reverse, carry):
        def body(step, cs):
            cs = list(cs)
            first = pl.multiple_of((NLAT // 8 - 1 - step if reverse else step) * 8, 8)
            decays = [latd_v[pl.ds(first, 8), lanes(h)] for h in HALF]
            for j in reversed(range(8)) if reverse else range(8):
                at = pl.ds(pl.multiple_of((first + j) * 8, 8), 8)
                for h in HALF:
                    d = decays[h][j:j + 1]
                    t = adj[h, at, :] + cs[h]
                    adj[h, at, :] = (1.0 - d) * t
                    cs[h] = d * t
            return tuple(cs)

        return lax.fori_loop(0, NLAT // 8, body, tuple(carry))

    carried = [adjoint(k % 2 == 0, [one_hot(k)] * 2) for k in (3, 2, 1, 0)]
    for h in HALF:
        e1, e2 = carried[3][h], carried[2][h]
        store_coefs(latco, (lat, h), 0, (e1[0:1], e1[1:2], e2[2:3], e1[2:3], e2[3:4], e1[3:4]))
    for k in FAR_LATS:
        send(latco.at[lat], latco.at[lat], 12, lat_peer(k))

    arrived(segco.at[other], 0)
    co = lambda s, h, r: segco[s, h, pl.ds(r, 1), :]

    def compose(left, right):
        g_l, a21_l, a32_l, a31_l, a42_l, a41_l = left
        g_r, a21_r, a32_r, a31_r, a42_r, a41_r = right
        b1 = a21_r * g_l
        f2 = a32_l * b1 + a31_l
        b2 = a21_r * f2 + a41_r * g_l
        f2b = a32_l * g_r
        return (
            g_l * g_r,
            g_l * b1 + a21_l,
            g_r * f2b + a32_r,
            g_r * f2 + a31_r * g_l,
            g_l * (a21_r * f2b + a42_r) + a42_l * g_r,
            g_l * b2 + a42_l * b1 + a41_l,
        )

    lon_sweeps(core, put_own)

    weights = [[[adj[h, pl.ds(256 * half + k, 32, stride=8), :] for k in STATES] for half in (core, other)] for h in HALF]
    for h in HALF:
        for c in STATES:
            own, rest = seg[core, h, c], pair_out[h, c]
            for k in STATES:
                total = weights[h][0][k] * own + weights[h][1][k] * rest
                latc[lat, h, pl.ds(4 * k + c, 1), :] = jnp.sum(total, axis=0, keepdims=True)
    for k in FAR_LATS:
        send(latc.at[lat], latc.at[lat], 7, lat_peer(k))

    arrived(seg.at[other], 1)
    def merge(h, left, right):
        g_l, a21_l, a32_l, a31_l, a42_l, a41_l = (co(0, h, r) for r in range(6))
        g_r, a21_r, a32_r, a31_r, a42_r, a41_r = (co(1, h, r) for r in range(6))
        (l1, l2, l3, l4), (r1, r2, r3, r4) = left, right
        b1 = a21_r * l1 + r2
        f2 = a32_l * b1 + l3
        b2 = a21_r * f2 + a41_r * l1 + r4
        return (
            g_r * l1 + r1,
            g_l * b1 + l2,
            g_r * f2 + a31_r * l1 + r3,
            g_l * b2 + a42_l * b1 + l4,
        )

    def unmerge(h, left, right, entering):
        g_l, a21_l, a32_l, a31_l, a42_l, a41_l = (co(0, h, r) for r in range(6))
        g_r, a21_r, a32_r, a31_r, a42_r, a41_r = (co(1, h, r) for r in range(6))
        (l1, l2, l3, l4), (r1, r2, r3, r4) = left, right
        e1, e2, e3, e4 = entering
        f1 = g_l * e1 + l1
        b1 = g_r * e2 + a21_r * f1 + r2
        f2 = g_l * e3 + a32_l * b1 + a31_l * e1 + l3
        b2 = g_r * e4 + a21_r * f2 + a42_r * e2 + a41_r * f1 + r4
        return (e1, b1, e3, b2), (f1, e2, f2, e4)

    states = lambda s, h: [seg[s, h, k] for k in STATES]
    for h in HALF:
        merged = merge(h, states(0, h), states(1, h))
        for k in STATES:
            for j in range(8):
                s_out[2 * j + h, k] = merged[k][4 * j:4 * j + 4]
    for k in FAR_CHIPS:
        send(s_out.at[chip_at(k)], s_in.at[CHIPS - k], 3, peer(k))
    s_in[0] = s_out[chip]

    latu[...] = jnp.zeros_like(latu)

    def lat_sweep(lines, reverse, carry):
        def body(step, ys):
            ys = list(ys)
            first = pl.multiple_of((NLAT // 8 - 1 - step if reverse else step) * 8, 8)
            decays = [latd_v[pl.ds(first, 8), lanes(h)] for h in HALF]
            for j in reversed(range(8)) if reverse else range(8):
                i = first + j
                for n, (ref, h, height) in enumerate(lines):
                    d = decays[h][j:j + 1]
                    at = pl.ds(pl.multiple_of(i * height, height), height)
                    ys[n] = d * ys[n] + (1.0 - d) * ref[h, at, :]
                    ref[h, at, :] = ys[n]
            return tuple(ys)

        return lax.fori_loop(0, NLAT // 8, body, tuple(carry))

    lines = [(work, 0, 16), (work, 1, 16), (latu, 0, 8), (latu, 1, 8)]
    ends = []
    for k in STATES:
        start = [jnp.zeros((16, LANES), F32)] * 2 + [one_hot(k)] * 2
        ends.append(lat_sweep(lines, k % 2 == 1, start))
    for n in range(LATS):
        for k in STATES:
            lz_out[n, k] = ends[k][n // 4][4 * (n % 4):4 * (n % 4) + 4]
    for k in FAR_LATS:
        send(lz_out.at[lax.rem(lat + k, LATS)], lz_in.at[lat], 4, lat_peer(k))
    lz_in[lat] = lz_out[lat]

    arrived(sc_in.at[core, pl.ds(1, CHIPS - 1)], 8)
    send(sc_in.at[core], sc_in.at[core], 2, partner)

    def lat_solve(state, coef, put, zero):
        x1, x2, x3, x4 = ([zero] * LATS for _ in STATES)
        for p in range(LATS - 1):
            x1[p + 1] = coef(p, 0) * x1[p] + state(p, 0)
        for p in range(LATS - 1, 0, -1):
            x2[p - 1] = coef(p, 0) * x2[p] + (coef(p, 1) * x1[p] + state(p, 1))
        for p in range(LATS - 1):
            x3[p + 1] = coef(p, 0) * x3[p] + (coef(p, 2) * x2[p] + coef(p, 3) * x1[p] + state(p, 2))
        for p in range(LATS - 1, 0, -1):
            x4[p - 1] = coef(p, 0) * x4[p] + (
                coef(p, 1) * x3[p] + coef(p, 4) * x2[p] + coef(p, 5) * x1[p] + state(p, 3)
            )
        for p in range(LATS):
            for k, x in enumerate((x1, x2, x3, x4)):
                put(p, k, x[p])

    arrived(latco.at[pl.ds(0, LATS - 1)], 12)
    arrived(latc.at[pl.ds(0, LATS - 1)], 7)
    for h in HALF:
        def put_c(p, k, x, h=h):
            latcx[p, h, pl.ds(4 * k, 4), :] = x

        lat_solve(
            lambda p, k: latc[p, h, pl.ds(4 * k, 4), :],
            lambda p, r: latco[p, h, pl.ds(r, 1), :],
            put_c, jnp.zeros((4, LANES), F32),
        )
    place = lambda k, h: k % 2 + 2 * h + 4 * (k // 2)
    for k in STATES:
        for h in HALF:
            t_out[place(k, h)] = latcx[lat, h, pl.ds(4 * k, 4), :]
    for k in FAR_LONS:
        send(t_out.at[lax.rem(lon + k, 8)], t_in.at[LONS - k], 9, lon_peer(k))
    t_in[0] = t_out[lax.rem(lon, 8)]

    seat = range(CHIPS)

    def ring_maps(cc):
        seat = range(len(cc))
        ahead, behind = [jnp.ones((1, LANES), F32)], [jnp.ones((1, LANES), F32)]
        for j in seat:
            ahead.append(ahead[-1] * cc[j][0])
            behind.append(behind[-1] * cc[-1 - j][0])
        return cc, ahead, behind, 1.0 / (1.0 - ahead[-1])

    def ring_solve(seat, maps, state, zero):
        cc, ahead, behind, close = maps

        def ring(terms, reverse):
            t = zero
            before = [None] * len(seat)
            for j in reversed(seat) if reverse else seat:
                before[j] = t
                t = cc[j][0] * t + terms[j]
            start = t * close
            growth = (lambda j: behind[len(seat) - 1 - j]) if reverse else (lambda j: ahead[j])
            return [before[j] + growth(j) * start for j in seat]

        x1 = ring([state(j, 0) for j in seat], False)
        x2 = ring([state(j, 1) + cc[j][1] * x1[j] for j in seat], True)
        x3 = ring([state(j, 2) + cc[j][3] * x1[j] + cc[j][2] * x2[j] for j in seat], False)
        x4 = ring([state(j, 3) + cc[j][5] * x1[j] + cc[j][4] * x2[j] + cc[j][1] * x3[j] for j in seat], True)
        return x1, x2, x3, x4

    arrived(sc_in.at[other], 2)
    rows = lambda c, j: [sc_in[c, j, pl.ds(r, 1), :] for r in range(6)]
    maps = ring_maps([compose(rows(0, j), rows(1, j)) for j in seat])
    arrived(s_in.at[pl.ds(1, CHIPS - 1)], 3)
    x1, x2, x3, x4 = ring_solve(seat, maps, lambda j, k: s_in[j, k], jnp.zeros((4, LANES), F32))
    for j in seat:
        for k, x in enumerate((x1, x2, x3, x4)):
            x_out[j, k] = x[j]
    for k in FAR_CHIPS:
        send(x_out.at[k], x_in.at[chip], 5, peer(k))
    x_in[chip] = x_out[0]

    devices = range(LONS)
    maps = ring_maps([rows(lax.rem(core + j, 2), lax.rem((core + j) // 2, CHIPS)) for j in devices])
    arrived(t_in.at[pl.ds(1, LONS - 1)], 9)
    found = ring_solve(devices, maps, lambda j, c: t_in[j, pl.ds(c, 1), :], jnp.zeros((1, LANES), F32))
    for j in devices:
        for c in STATES:
            tx_out[j, pl.ds(c, 1), :] = found[c][j]
    for k in range(1, 8):
        near = 8 * (lon // 8) + lax.rem(lon + k, 8)
        send(tx_out.at[lax.rem(near - lon + LONS, LONS)], tx_in.at[lax.rem(lon, 8)], 10, {"lon": near})
    tx_in[lax.rem(lon, 8)] = tx_out[0]

    arrived(lz_in.at[pl.ds(0, LATS - 1)], 4)

    def put_z(p, k, x):
        lzx_out[p, k] = x

    lat_solve(
        lambda p, k: lz_in[p, k],
        lambda p, r: latco[p, lat // 4, pl.ds(r, 1), :],
        put_z, jnp.zeros((4, LANES), F32),
    )
    for k in FAR_LATS:
        send(lzx_out.at[lax.rem(lat + k, LATS)], lzx_in.at[lat], 11, lat_peer(k))
    lzx_in[lat] = lzx_out[lat]

    arrived(x_in.at[pl.ds(0, CHIPS - 1)], 5)
    for h in HALF:
        entering = [jnp.concatenate([x_in[2 * j + h, k] for j in range(8)], axis=0) for k in STATES]
        for whose, parts_in in enumerate(unmerge(h, states(0, h), states(1, h), entering)):
            for k in STATES:
                unm[whose, h, k] = parts_in[k]
    send(unm.at[other], xlon.at[core], 6, partner)

    xlon[core] = unm[core]
    xcol[...] = jnp.zeros_like(xcol)
    arrived(xlon.at[other], 6)
    for h in HALF:
        for half in range(2):
            for c in STATES:
                xcol[h, pl.ds(256 * half + c, 32, stride=8), :] = xlon[half, h, c]
    lines = [(xcol, 0, 8), (xcol, 1, 8)]
    for k in STATES:
        lat_sweep(lines, k % 2 == 1, [jnp.zeros((8, LANES), F32)] * 2)
    lon_unit = [[lonu[h, pl.ds(c, NLON, stride=8), :] for c in STATES] for h in HALF]

    def add_lon(step, _):
        for j in range(4):
            i = step * 4 + j
            for h in HALF:
                at = pl.ds(pl.multiple_of(i * 16, 16), 16)
                y = work[h, at, :]
                column = xcol[h, pl.ds(pl.multiple_of(i * 8, 8), 8), :]
                for c in STATES:
                    y = y + column[c:c + 1] * lon_unit[h][c]
                work[h, at, :] = y
        return 0

    lax.fori_loop(0, NLAT // 4, add_lon, 0)

    arrived(lzx_in.at[pl.ds(0, LATS - 1)], 11)

    arrived(tx_in.at[pl.ds(0, 7)], 10)
    for h in HALF:
        for k in STATES:
            x = jnp.concatenate([lzx_in[4 * h + g, k] for g in range(4)], axis=0)
            for c in STATES:
                x = x + lon_unit[h][c] * tx_in[place(k, h), pl.ds(c, 1), :]
            enter[h, k] = x

    sent(segco.at[core], 0)
    sent(pair_out, 1)
    sent(s_in.at[pl.ds(1, CHIPS - 1)], 3)
    sent(lz_in.at[pl.ds(0, LATS - 1)], 4)
    sent(x_in.at[pl.ds(0, CHIPS - 1)], 5)
    sent(unm.at[other], 6)
    sent(latc.at[pl.ds(0, LATS - 1)], 7)
    sent(latco.at[pl.ds(0, LATS - 1)], 12)
    sent(lzx_in.at[pl.ds(0, LATS - 1)], 11)

    sent(sc_in.at[core], 2)
    sent(sc_in.at[core, pl.ds(1, CHIPS - 1)], 8)
    sent(t_in.at[pl.ds(1, LONS - 1)], 9)
    sent(tx_in.at[pl.ds(0, 7)], 10)


def finish(work, latu, enter, std, tw, out, line, out_v, sem):
    parts = 8
    size = ROWS // parts

    for step in range(parts):
        rows = pl.ds(step * size, size)
        for h in HALF:
            for j in range(size // 16):
                i = step * (size // 16) + j
                y = work[h, pl.ds(i * 16, 16), :]
                unit = latu[h, pl.ds(i * 8, 8), :]
                for k in STATES:
                    y = y + unit[k:k + 1] * enter[h, k]
                line[h, pl.ds(16 * j, 16), :] = y
            lanes = pl.ds(h * LANES, LANES)
            out_v[rows, lanes] = std[rows, lanes] * dot3(line[h], tw[h])
        pltpu.make_async_copy(out_v.at[rows], out.at[rows], sem.at[0]).start()

    pltpu.make_async_copy(out_v, out, sem.at[0]).wait()


def per_device(increment, error_std, vertical, lon_decay, lat_decay):
    vmem = lambda *shape: pltpu.VMEM(shape, F32)
    whole = pl.BlockSpec(memory_space=pltpu.VMEM)
    weights = pltpu.VMEM((2, 256, 256), BF16)
    held = pl.pallas_call(
        kernel,
        out_shape=[
            vmem(2, ROWS, LANES), vmem(2, NLAT * 8, LANES), vmem(2, 4, NLON, LANES), vmem(ROWS, 256), weights,
        ],
        in_specs=[pl.BlockSpec(memory_space=pl.ANY)] * 5,
        out_specs=[whole] * 5,
        scratch_shapes=[
            vmem(ROWS, 256), vmem(4, 64, 64), vmem(NLON, 256), vmem(NLAT, 256),
            weights, vmem(2, NLON, 32, LANES), vmem(2, NLON * 8, LANES),
            *[vmem(2, NLAT * 8, LANES)] * 2,
            vmem(2, 4, 32, LANES), vmem(2, 2, 4, 32, LANES), vmem(2, 2, 8, LANES),
            *[vmem(CHIPS, 4, 4, LANES)] * 4,
            vmem(2, 2, 4, 32, LANES), vmem(2, 2, 4, 32, LANES),
            vmem(LATS, 2, 16, LANES), vmem(LATS, 2, 8, LANES), vmem(LATS, 2, 16, LANES), *[vmem(LATS, 4, 4, LANES)] * 4,
            vmem(2, CHIPS, 8, LANES), vmem(8, 4, LANES), vmem(LONS, 4, LANES), vmem(LONS, 4, LANES), vmem(8, 4, LANES),
            pltpu.SemaphoreType.DMA((11,)), pltpu.SemaphoreType.DMA((13,)), pltpu.SemaphoreType.DMA((13,)),
        ],
        compiler_params=pltpu.CompilerParams(
            collective_id=0, has_side_effects=True, vmem_limit_bytes=24 * 1024 * 1024
        ),
    )(*[
        pltpu.with_memory_space_constraint(x, pltpu.HBM)
        for x in (increment.reshape(ROWS, 256), error_std.reshape(ROWS, 256), vertical, lon_decay, lat_decay)
    ])
    result = pl.pallas_call(
        finish,
        out_shape=jax.ShapeDtypeStruct((ROWS, 256), F32),
        in_specs=[whole] * 5,
        out_specs=pl.BlockSpec(memory_space=pl.ANY),
        scratch_shapes=[vmem(2, ROWS // 8, LANES), vmem(ROWS, 256), pltpu.SemaphoreType.DMA((1,))],
        compiler_params=pltpu.CompilerParams(vmem_limit_bytes=24 * 1024 * 1024),
    )(*held)
    return result.reshape(NLAT, NLON, 256)


def solution(mesh):
    placed = (P("lat", "lon", None), P("lat", "lon", None), P(), P("lon", None), P("lat", None))
    return jax.shard_map(
        per_device, mesh=mesh, in_specs=placed, out_specs=P("lat", "lon", None), check_vma=False
    )
```
